128 devices in a mesh: gx: 16 (over x, y), gy: 8 (over z, core).
Axes of the slice: x: 4, y: 4, z: 4, core: 2. Of those that a mesh axis runs over, the one named last changes fastest.
Arguments:
- populations: float32 [19, 256, 32, 1024], P(None, ('gx', 'gy')), may hold values from 0.5 to 1.5
- concentration: float32 [2, 256, 32, 1024], P(None, ('gx', 'gy')), may hold values from 0.5 to 2
- potential: float32 [256, 32, 1024], P(('gx', 'gy')), may hold values from -5.4 to 5.4
- mobility: float32 [256, 32, 1024], P(('gx', 'gy')), may hold values from 0.3 to 1.5
- solid_mask: int32 [256, 32, 1024], P(('gx', 'gy')), may hold values 0 or 1
- block_col: int32 [256], replicated, may hold values from 0 to 31, as said below
Outputs:
- populations_next: float32 [19, 256, 32, 1024], P(None, ('gx', 'gy'))
- concentration_next: float32 [2, 256, 32, 1024], P(None, ('gx', 'gy'))
- potential_next: float32 [256, 32, 1024], P(('gx', 'gy'))
The draws below stay inside these ranges and needn't reach their ends.
Inputs may be any that keep to these rules, and one draw needn't show every extreme that they name: `block_col`: slot t = ((N i + j) * 2 + k), for device i along gx, j along gy, N devices along gy and k < 2, holds the block of row j at column (2 i + s_j + k) mod 32, where every row j has one start s_j with 0 <= s_j < 2; not all rows have the same start.
All inputs are finite; a program needn't handle non-finite values. No bound on the sum of `solid_mask` on one device may be relied on, other than what follows from the above.
Results may differ from the reference program's by a relative error of at most 0.0003.
Values sent between devices are 32-bit elements; how exact they have to be, the bound alone decides.
A program may use at most 128 MiB of HBM per device.

```python
import math
import jax
import jax.numpy as jnp

BS = 32
Q = 19
SPECIES = 2
ITERS = 2
STEPS = 4
BLK_DEV = 2
NB = 256
GBX = 32
NXG = 1024
NYG = 256
N_GX = 16
N_GY = 8


def draw_block_col(key, part):
    key = jax.random.fold_in(key, 11)
    row_offsets = jax.random.randint(key, (N_GY,), 0, BLK_DEV)
    row_offsets = row_offsets.at[0].set((row_offsets[1] + 1) % BLK_DEV)
    slot_index = jnp.arange(NB, dtype=jnp.int32)
    device = slot_index // BLK_DEV
    across = device // N_GY
    row_number = device % N_GY
    within = slot_index % BLK_DEV
    return ((BLK_DEV * across + row_offsets[row_number] + within) % GBX).astype(jnp.int32)


def draw_potential(key, part):
    key = jax.random.fold_in(key, 23)
    key_block, key_column, key_sample = jax.random.split(key, 3)
    slot_index = jnp.arange(NB, dtype=jnp.float32)
    rising = 1.0 + 2.0 * slot_index / (NB - 1)
    block_scale = jnp.exp(jax.random.uniform(key_block, (NB,), minval=0.0, maxval=math.log(10.0)))
    column_scale = jnp.exp(jax.random.uniform(key_column, (NB, BS, 1), minval=0.0, maxval=math.log(3.0)))
    overall = (rising * block_scale)[:, None, None] * column_scale
    sample = jax.random.truncated_normal(key_sample, -4.0, 4.0, (NB, BS, BS * BS))
    return (0.015 * overall * sample).astype(jnp.float32)


def touch_ends(array, stream_key, least, top_value):
    extent = array.shape
    place = [jax.random.randint(jax.random.fold_in(stream_key, axis), (), 0, extent[axis]) for axis in range(len(extent))]
    array = array.at[tuple(place)].set(least)
    longest = extent.index(max(extent))
    place[longest] = (place[longest] + 1) % extent[longest]
    return array.at[tuple(place)].set(top_value)


def block_levels(stream_key, dims, shards, least, high):
    loudness, own = 1.0, jax.random.fold_in(stream_key, 6)
    for axis_at, blocks in shards:
        steps = jnp.exp(jax.random.uniform(jax.random.fold_in(own, axis_at), (blocks,), jnp.float32, least / len(shards), high / len(shards)))
        loudness = loudness * jnp.repeat(steps, dims[axis_at] // blocks).reshape([-1 if axis == axis_at else 1 for axis in range(len(dims))])
    return loudness


def setup_inputs(seed: int = 0) -> dict:
    key_list = jax.random.split(jax.random.key(seed), 7)
    populations = jnp.clip(0.5 + 1.0 * jax.random.uniform(key_list[0], (Q, NB, BS, BS * BS), jnp.float32) ** block_levels(key_list[0], (Q, NB, BS, BS * BS), ((1, 128),), -0.2, 0.2), 0.5, 1.5)
    concentration = jnp.clip(0.5 + 1.5 * jax.random.uniform(key_list[1], (SPECIES, NB, BS, BS * BS), jnp.float32) ** block_levels(key_list[1], (SPECIES, NB, BS, BS * BS), ((1, 128),), -0.2, 0.2), 0.5, 2.0)
    potential = draw_potential(jax.random.fold_in(key_list[6], 71), 0)
    mobility = jnp.clip(jnp.exp(math.log(1.5) - 1.60943787 * jax.random.uniform(key_list[3], (NB, BS, BS * BS), jnp.float32) ** block_levels(key_list[3], (NB, BS, BS * BS), ((0, 128),), -0.2, 0.2)), 0.3, 1.5)
    solid_mask = touch_ends((jax.random.randint(key_list[4], (NB, BS, BS * BS), 0, 5) < 2).astype(jnp.int32), jax.random.fold_in(key_list[4], 1), 0, 1)
    block_col = draw_block_col(jax.random.fold_in(key_list[6], 71), 0)
    return dict(populations=populations, concentration=concentration, potential=potential, mobility=mobility, solid_mask=solid_mask, block_col=block_col)


VELOCITY = ((0, 0, 0), (1, 0, 0), (-1, 0, 0), (0, 1, 0), (0, -1, 0), (0, 0, 1), (0, 0, -1),
            (1, 1, 0), (-1, -1, 0), (1, -1, 0), (-1, 1, 0), (1, 0, 1), (-1, 0, -1), (1, 0, -1),
            (-1, 0, 1), (0, 1, 1), (0, -1, -1), (0, 1, -1), (0, -1, 1))
OPPOSITE = (0, 2, 1, 4, 3, 6, 5, 8, 7, 10, 9, 12, 11, 14, 13, 16, 15, 18, 17)
LATTICE_WEIGHT = (1.0 / 3.0,) + (1.0 / 18.0,) * 6 + (1.0 / 36.0,) * 12
RELAX_TIME = 0.8
SCREENING = 0.5
APPLIED = 0.4
ION_STEP = 0.05
PECLET = 1.0
FORCE_SCALE = 0.5
VALENCE = (1.0, -1.0)


def forward_value(values, axis_index):
    if axis_index < 2:
        return jnp.roll(values, -1, axis_index)
    return jnp.concatenate([values[:, :, 1:], jnp.zeros_like(values[:, :, :1])], 2)


def backward_value(values, axis_index):
    if axis_index < 2:
        return jnp.roll(values, 1, axis_index)
    return jnp.concatenate([jnp.zeros_like(values[:, :, :1]), values[:, :, :-1]], 2)


def slot_places(block_col):
    column = block_col.reshape(N_GX, N_GY, BLK_DEV)
    row_index = jnp.broadcast_to(jnp.arange(N_GY, dtype=jnp.int32)[None, :, None], column.shape)
    return column, row_index


def to_grid(values, block_col):
    blocks_view = values.reshape(N_GX, N_GY, BLK_DEV, BS, BS, BS)
    column, row_index = slot_places(block_col)
    dense = jnp.zeros((GBX, N_GY, BS, BS, BS), values.dtype)
    dense = dense.at[column, row_index].set(blocks_view)
    return dense.transpose(0, 2, 1, 3, 4).reshape(NXG, NYG, BS)


def from_grid(dense, block_col):
    blocks_view = dense.reshape(GBX, BS, N_GY, BS, BS).transpose(0, 2, 1, 3, 4)
    column, row_index = slot_places(block_col)
    return blocks_view[column, row_index].reshape(NB, BS, BS * BS)


def operate(values, transport, diagonal):
    result = diagonal * values
    for axis_index in range(3):
        face_term = (transport * forward_value(transport, axis_index)) * (values - forward_value(values, axis_index))
        result = result + face_term - backward_value(face_term, axis_index)
    return result


def face_flux(coeff_a, coeff_b, conc_a, conc_b, pot_a, pot_b, vel_a, vel_b, valence, applied):
    mean_conc = 0.5 * (conc_a + conc_b)
    potential_drop = pot_b - pot_a - applied
    face_velocity = 0.5 * (vel_a + vel_b)
    return (coeff_a * coeff_b) * ((conc_a - conc_b) - valence * mean_conc * potential_drop + PECLET * face_velocity * mean_conc)


def body_force(charge, slope_x, slope_y):
    return [FORCE_SCALE * charge * (APPLIED - slope_x), FORCE_SCALE * charge * (0.0 - slope_y), jnp.zeros_like(charge)]


def moments(pop_list):
    density = pop_list[0]
    for pop_index in range(1, len(pop_list)):
        density = density + pop_list[pop_index]
    velocity = []
    for axis_index in range(3):
        momentum = None
        for pop_index in range(len(pop_list)):
            component = VELOCITY[pop_index][axis_index]
            if component != 0:
                signed_pop = pop_list[pop_index] if component > 0 else -pop_list[pop_index]
                momentum = signed_pop if momentum is None else momentum + signed_pop
        velocity.append(momentum / density)
    return density, velocity


def collide(pop_list, density, velocity, body_push, fluid_flag):
    shifted = [velocity[axis_index] + RELAX_TIME * body_push[axis_index] / density for axis_index in range(3)]
    square = shifted[0] * shifted[0] + shifted[1] * shifted[1] + shifted[2] * shifted[2]
    post_list = []
    for pop_index in range(len(pop_list)):
        projection = jnp.zeros_like(density)
        for axis_index in range(3):
            component = VELOCITY[pop_index][axis_index]
            if component > 0:
                projection = projection + shifted[axis_index]
            elif component < 0:
                projection = projection - shifted[axis_index]
        equilibrium = LATTICE_WEIGHT[pop_index] * density * (1.0 + 3.0 * projection + 4.5 * projection * projection - 1.5 * square)
        relaxed = pop_list[pop_index] - (pop_list[pop_index] - equilibrium) / RELAX_TIME
        post_list.append(jnp.where(fluid_flag, relaxed, pop_list[OPPOSITE[pop_index]]))
    return post_list


def propagate(post_list, depth_index):
    result = []
    for pop_index in range(len(post_list)):
        step_x, step_y, step_z = VELOCITY[pop_index]
        shifted = jnp.roll(post_list[pop_index], (step_x, step_y), axis=(0, 1))
        if step_z == 1:
            shifted = backward_value(shifted, 2)
        elif step_z == -1:
            shifted = forward_value(shifted, 2)
        inside = (depth_index - step_z >= 0) & (depth_index - step_z < BS)
        result.append(jnp.where(inside, shifted, post_list[OPPOSITE[pop_index]]))
    return result


def reference(populations, concentration, potential, mobility, solid_mask, block_col):
    pop_list = [to_grid(populations[pop_index], block_col) for pop_index in range(Q)]
    ion_conc = [to_grid(concentration[species], block_col) for species in range(SPECIES)]
    phi_field = to_grid(potential, block_col)
    fluid_flag = to_grid(solid_mask, block_col) == 0
    fluid_value = fluid_flag.astype(potential.dtype)
    transport = to_grid(mobility, block_col) * fluid_value
    diagonal = SCREENING * fluid_value + (1.0 - fluid_value)
    depth_index = jnp.arange(BS, dtype=jnp.int32)[None, None, :]
    for step_index in range(STEPS):
        density, velocity = moments(pop_list)
        source = fluid_value * (ion_conc[0] - ion_conc[1])
        residual = source - operate(phi_field, transport, diagonal)
        direction = residual
        norm_now = jnp.sum(residual * residual)
        for iteration in range(ITERS):
            mapped = operate(direction, transport, diagonal)
            step_length = norm_now / jnp.sum(direction * mapped)
            phi_field = phi_field + step_length * direction
            residual = residual - step_length * mapped
            if iteration + 1 < ITERS:
                norm_next = jnp.sum(residual * residual)
                direction = residual + (norm_next / norm_now) * direction
                norm_now = norm_next
        updated = []
        for species in range(SPECIES):
            divergence = jnp.zeros_like(phi_field)
            conc_now = ion_conc[species]
            for axis_index in range(3):
                applied = APPLIED if axis_index == 0 else 0.0
                face_term = face_flux(transport, forward_value(transport, axis_index), conc_now,
                                      forward_value(conc_now, axis_index), phi_field,
                                      forward_value(phi_field, axis_index), velocity[axis_index],
                                      forward_value(velocity[axis_index], axis_index), VALENCE[species], applied)
                divergence = divergence + face_term - backward_value(face_term, axis_index)
            updated.append(conc_now - ION_STEP * divergence)
        ion_conc = updated
        charge = ion_conc[0] - ion_conc[1]
        slope_x = 0.5 * (forward_value(phi_field, 0) - backward_value(phi_field, 0))
        slope_y = 0.5 * (forward_value(phi_field, 1) - backward_value(phi_field, 1))
        body_push = body_force(charge, slope_x, slope_y)
        post_list = collide(pop_list, density, velocity, body_push, fluid_flag)
        pop_list = propagate(post_list, depth_index)
    pop_out = jnp.stack([from_grid(pop_value, block_col) for pop_value in pop_list], 0)
    conc_out = jnp.stack([from_grid(conc_value, block_col) for conc_value in ion_conc], 0)
    return pop_out, conc_out, from_grid(phi_field, block_col)
```

```python
import jax
import jax.numpy as jnp
from jax import lax
from jax.experimental import pallas as pl
from jax.experimental.pallas import tpu as pltpu
from jax.sharding import PartitionSpec as P

BS = 32
Q = 19
STEPS = 4
N_GX = 16
N_GY = 8
N_DEV = N_GX * N_GY
VELOCITY = (
    (0, 0, 0),
    (1, 0, 0),
    (-1, 0, 0),
    (0, 1, 0),
    (0, -1, 0),
    (0, 0, 1),
    (0, 0, -1),
    (1, 1, 0),
    (-1, -1, 0),
    (1, -1, 0),
    (-1, 1, 0),
    (1, 0, 1),
    (-1, 0, -1),
    (1, 0, -1),
    (-1, 0, 1),
    (0, 1, 1),
    (0, -1, -1),
    (0, 1, -1),
    (0, -1, 1),
)
OPPOSITE = (0, 2, 1, 4, 3, 6, 5, 8, 7, 10, 9, 12, 11, 14, 13, 16, 15, 18, 17)
UP_Y = (3, 7, 10, 15, 17)
DOWN_Y = (4, 8, 9, 16, 18)
UP_X = (1, 7, 9, 11, 13)
DOWN_X = (2, 8, 10, 12, 14)
RELAX_TIME = 0.8
SCREENING = 0.5
APPLIED = 0.4
ION_STEP = 0.05
FORCE_SCALE = 0.5

MESH = pl.DeviceIdType.MESH
LANES = 128
TILES = 8
ROWS = 64
EDGE = 16
NR = ROWS + 2 * EDGE
NT = TILES + 2
SIDE = 40
STRIP = ROWS + 2 * SIDE


def tile_offsets():
    hops = lambda a: min(a, 4 - a)
    offs = [
        (a, b, c, d)
        for a in range(4)
        for b in range(4)
        for c in range(4)
        for d in range(2)
        if a + b + c + d
    ]
    offs.sort(key=lambda o: -(hops(o[0]) + hops(o[1]) + hops(o[2]) + 0.1 * o[3]))
    return offs


def kernel(
    col_ref, pop_hbm, conc_hbm, pot_hbm, mob_hbm, mask_hbm,
    pop_out, conc_out, pot_out,
    f, g, phi, r0, w, aw, c, t, kx, ky, kym, kz, kzm, dg, fl, mk,
    ux, uy, uz, rho, rinv, vx, vy, flux,
    ar, sy_r, ry_r, sx_r, rx_r, sy_g, ry_g, sx_g, rx_g, sx_u, ry_u, rx_u,
    in_sem, out_sem, ar_send, ar_recv, send_r, recv_r, send_g, recv_g, send_u, recv_u,
):
    gx = lax.axis_index("gx")
    gy = lax.axis_index("gy")
    right = lax.rem(gx + 1, N_GX)
    left = lax.rem(gx + N_GX - 1, N_GX)
    above = lax.rem(gy + 1, N_GY)
    below = lax.rem(gy + N_GY - 1, N_GY)
    me = gx * N_GY + gy

    lane = lax.broadcasted_iota(jnp.int32, (8, LANES), 1)
    depth = lane % BS
    group = lane // BS
    z_first = depth == 0
    z_last = depth == BS - 1

    def in_copies():
        first = []
        pops = []
        for b in range(2):
            for j in range(TILES):
                lanes = pl.ds(j * LANES, LANES)
                rows = pl.ds(EDGE + b * BS, BS)
                own = pl.ds(b * BS, BS)
                first.append((pot_hbm.at[b, :, lanes], phi.at[1 + j, rows, :], 0))
                first.append((mob_hbm.at[b, :, lanes], t.at[1 + j, rows, :], 0))
                first.append((mask_hbm.at[b, :, lanes], mk.at[j, own, :], 0))
                first.append((conc_hbm.at[:, b, :, lanes], c.at[0, :, 1 + j, rows, :], 0))
                pops.append((pop_hbm.at[:, b, :, lanes], f.at[:, j, own, :], 1))
        return first, pops

    first, pops = in_copies()
    first = [pltpu.make_async_copy(s, d, in_sem.at[0, n]) for n, (s, d, k) in enumerate(first)]
    pops = [pltpu.make_async_copy(s, d, in_sem.at[1, n]) for n, (s, d, k) in enumerate(pops)]
    for copy in first:
        copy.start()
    for copy in pops:
        copy.start()

    barrier = pltpu.get_barrier_semaphore()

    def greet(k, _):
        other = lax.rem(me + k, N_DEV)
        pl.semaphore_signal(
            barrier, inc=1, device_id=(other // N_GY, lax.rem(other, N_GY)), device_id_type=MESH
        )
        return 0

    lax.fori_loop(1, N_DEV, greet, 0)

    def exchange(par, strip_src, strip_dst, x_src, x_dst, send, recv):
        copies = []
        for to_y, dst_side in ((below, 1), (above, 0)):
            src_side = 1 - dst_side
            for to_x, src_row, dst_row, count in (
                (gx, 0, SIDE, ROWS),
                (right, ROWS - SIDE, 0, SIDE),
                (left, 0, SIDE + ROWS, SIDE),
            ):
                copies.append(
                    (
                        strip_src(src_side, src_row, count),
                        strip_dst.at[par, dst_side, :, pl.ds(dst_row, count), :],
                        (to_x, to_y),
                    )
                )
        copies.append((x_src.at[1], x_dst.at[par, 0], (right, gy)))
        copies.append((x_src.at[0], x_dst.at[par, 1], (left, gy)))
        return [
            pltpu.make_async_remote_copy(
                src_ref=s, dst_ref=d, send_sem=send.at[k], recv_sem=recv.at[par, k],
                device_id=dev, device_id_type=MESH,
            )
            for k, (s, d, dev) in enumerate(copies)
        ]

    def staged(ref):
        return lambda side, row, count: ref.at[side, :, pl.ds(row, count), :]

    def ex_r(par):
        return exchange(par, staged(sy_r), ry_r, sx_r, rx_r, send_r, recv_r)

    def ex_g(par):
        return exchange(par, staged(sy_g), ry_g, sx_g, rx_g, send_g, recv_g)

    def ex_u(par):
        def src(side, row, count):
            tile = TILES if side == 1 else 1
            return uy.at[pl.ds(tile, 1), pl.ds(EDGE + row, count), :]

        return exchange(par, src, ry_u, sx_u, rx_u, send_u, recv_u)

    def start(copies):
        for copy in copies:
            copy.start()

    def finish(copies):
        for copy in copies:
            copy.wait()

    here = col_ref[2 * gy]
    ahead = [
        jnp.broadcast_to(here - col_ref[2 * other], (8, LANES)) for other in (below, above)
    ]
    less = [v < 0 for v in ahead]
    more = [v > 0 for v in ahead]

    def strip_rows(ref, par, side, number, k):
        first, same, last = [
            ref[par, side, number, pl.ds(start + 8 * k, 8), :] for start in (0, BS, 2 * BS)
        ]
        return jnp.where(less[side], first, jnp.where(more[side], last, same))

    def own_rows(step):
        return pl.multiple_of(EDGE + 8 * step, 8)

    def rolled(v, shift):
        return pltpu.roll(v, shift % LANES, 1)

    def y_next(v, tile, cache):
        if tile not in cache:
            cache[tile] = rolled(v[tile], -BS)
        if tile + 1 not in v:
            return cache[tile]
        if tile + 1 not in cache:
            cache[tile + 1] = rolled(v[tile + 1], -BS)
        return jnp.where(group < 3, cache[tile], cache[tile + 1])

    def y_prev(v, tile, cache):
        if tile not in cache:
            cache[tile] = rolled(v[tile], BS)
        if tile - 1 not in v:
            return cache[tile]
        if tile - 1 not in cache:
            cache[tile - 1] = rolled(v[tile - 1], BS)
        return jnp.where(group > 0, cache[tile], cache[tile - 1])

    def apply(ref, r, tiles, sink):
        rows = pl.ds(r, 8)
        low = max(0, tiles[0] - 1)
        high = min(NT - 1, tiles[-1] + 1)
        v = {j: ref[j, rows, :] for j in range(low, high + 1)}
        up = {}
        down = {}
        for j in tiles:
            here_v = v[j]
            out = dg[j, rows, :] * here_v
            out = out - kx[j, rows, :] * ref[j, pl.ds(r + 1, 8), :]
            out = out - kx[j, pl.ds(r - 1, 8), :] * ref[j, pl.ds(r - 1, 8), :]
            out = out - ky[j, rows, :] * y_next(v, j, up)
            out = out - kym[j, rows, :] * y_prev(v, j, down)
            out = out - kz[j, rows, :] * rolled(here_v, -1)
            out = out - kzm[j, rows, :] * rolled(here_v, 1)
            sink(j, here_v, out)

    OWN = list(range(1, TILES + 1))
    ALL = list(range(NT))

    def moments(pop):
        p = pop
        xp = p[7] + p[9] + p[11] + p[13] + p[1]
        xm = p[8] + p[10] + p[12] + p[14] + p[2]
        yp = p[15] + p[17] + p[3]
        ym = p[16] + p[18] + p[4]
        density = p[0] + xp + xm + yp + ym + (p[5] + p[6])
        jx = xp - xm
        jy = (yp - ym) + ((p[7] + p[10]) - (p[8] + p[9]))
        jz = (p[5] - p[6]) + ((p[11] + p[14]) - (p[12] + p[13])) + (
            (p[15] + p[18]) - (p[16] + p[17])
        )
        inverse = 1.0 / density
        return density, inverse, jx * inverse, jy * inverse, jz * inverse

    def store_moments(pop, j, r):
        density, inverse, a, b, d = moments(pop)
        rows = pl.ds(r, 8)
        own = pl.ds(pl.multiple_of(r - EDGE, 8), 8)
        rho[j - 1, own, :] = density
        rinv[j - 1, own, :] = inverse
        ux[j, rows, :] = a
        uy[j, rows, :] = b
        uz[j - 1, own, :] = d

    def send_velocity(par):
        for j in OWN:
            sx_u[0, 0, pl.ds(j - 1, 1), :] = ux[j, pl.ds(EDGE, 1), :]
            sx_u[1, 0, pl.ds(j - 1, 1), :] = ux[j, pl.ds(EDGE + ROWS - 1, 1), :]
        start(ex_u(par))

    def take_velocity(par):
        finish(ex_u(par))
        for j in OWN:
            ux[j, pl.ds(EDGE - 1, 1), :] = rx_u[par, 0, 0, pl.ds(j - 1, 1), :]
            ux[j, pl.ds(EDGE + ROWS, 1), :] = rx_u[par, 1, 0, pl.ds(j - 1, 1), :]
        for k in range(10):
            rows = pl.ds(EDGE - 8 + 8 * k, 8)
            uy[0, rows, :] = strip_rows(ry_u, par, 0, 0, k)
            uy[NT - 1, rows, :] = strip_rows(ry_u, par, 1, 0, k)

    def send_residual(par, cp):
        for k in range(8):
            rows = pl.ds(EDGE + 8 * k, 8)
            out = pl.ds(8 * k, 8)
            v = r0[1, rows, :]
            a = rolled(c[cp, 0, 1, rows, :], 2 * BS)
            b = rolled(c[cp, 1, 1, rows, :], 3 * BS)
            sy_r[0, 0, out, :] = jnp.where(group < 2, v, jnp.where(group == 2, a, b))
            v = r0[TILES, rows, :]
            a = rolled(c[cp, 0, TILES, rows, :], BS)
            b = rolled(c[cp, 1, TILES, rows, :], 2 * BS)
            sy_r[1, 0, out, :] = jnp.where(group > 1, v, jnp.where(group == 0, a, b))
        for j in OWN:
            to = pl.ds(j - 1, 1)
            last = EDGE + ROWS - 1
            sx_r[0, 0, to, :] = r0[j, pl.ds(EDGE, 1), :]
            sx_r[0, 1, to, :] = r0[j, pl.ds(EDGE + 1, 1), :]
            sx_r[1, 0, to, :] = r0[j, pl.ds(last, 1), :]
            sx_r[1, 1, to, :] = r0[j, pl.ds(last - 1, 1), :]
            for s in range(2):
                sx_r[0, 2 + s, to, :] = c[cp, s, j, pl.ds(EDGE, 1), :]
                sx_r[1, 2 + s, to, :] = c[cp, s, j, pl.ds(last, 1), :]
        start(ex_r(par))

    def take_residual(par, cp):
        finish(ex_r(par))
        for k in range(10):
            rows = pl.ds(EDGE - 8 + 8 * k, 8)
            v = strip_rows(ry_r, par, 0, 0, k)
            r0[0, rows, :] = v
            c[cp, 0, 0, rows, :] = rolled(v, 3 * BS)
            c[cp, 1, 0, rows, :] = rolled(v, 2 * BS)
            v = strip_rows(ry_r, par, 1, 0, k)
            r0[NT - 1, rows, :] = v
            c[cp, 0, NT - 1, rows, :] = rolled(v, 2 * BS)
            c[cp, 1, NT - 1, rows, :] = rolled(v, BS)
        for j in OWN:
            at = pl.ds(j - 1, 1)
            last = EDGE + ROWS - 1
            r0[j, pl.ds(EDGE - 1, 1), :] = rx_r[par, 0, 0, at, :]
            r0[j, pl.ds(EDGE - 2, 1), :] = rx_r[par, 0, 1, at, :]
            r0[j, pl.ds(last + 1, 1), :] = rx_r[par, 1, 0, at, :]
            r0[j, pl.ds(last + 2, 1), :] = rx_r[par, 1, 1, at, :]
            for s in range(2):
                c[cp, s, j, pl.ds(EDGE - 1, 1), :] = rx_r[par, 0, 2 + s, at, :]
                c[cp, s, j, pl.ds(last + 1, 1), :] = rx_r[par, 1, 2 + s, at, :]

    def send_populations(par):
        for side, tile, names in ((0, 1, DOWN_Y), (1, TILES, UP_Y)):
            home = 0 if side == 0 else 3
            for k in range(8):
                rows = pl.ds(EDGE + 8 * k, 8)
                out = pl.ds(8 * k, 8)
                parts = [
                    rolled(g[q, tile, rows, :], (at % 4 - home) * BS)
                    for at, q in enumerate(names)
                ]
                sy_g[side, 0, out, :] = jnp.where(
                    group == 0, parts[0],
                    jnp.where(group == 1, parts[1], jnp.where(group == 2, parts[2], parts[3])),
                )
                sy_g[side, 1, out, :] = parts[4]
        for side, row, names in ((0, EDGE, DOWN_X), (1, EDGE + ROWS - 1, UP_X)):
            for at, q in enumerate(names):
                for j in OWN:
                    sx_g[side, at, pl.ds(j - 1, 1), :] = g[q, j, pl.ds(row, 1), :]
        start(ex_g(par))

    def take_populations(par):
        finish(ex_g(par))
        for side, tile, names in ((0, 0, UP_Y), (1, NT - 1, DOWN_Y)):
            home = 3 if side == 0 else 0
            for k in range(10):
                rows = pl.ds(EDGE - 8 + 8 * k, 8)
                v = strip_rows(ry_g, par, side, 0, k)
                for at, q in enumerate(names):
                    if at == 4:
                        v = strip_rows(ry_g, par, side, 1, k)
                    g[q, tile, rows, :] = rolled(v, (home - at % 4) * BS)
        for side, row, names in ((0, EDGE - 1, UP_X), (1, EDGE + ROWS, DOWN_X)):
            for at, q in enumerate(names):
                for j in OWN:
                    g[q, j, pl.ds(row, 1), :] = rx_g[par, side, at, pl.ds(j - 1, 1), :]

    def propagate(with_moments):
        @pl.loop(0, 8)
        def _(step):
            r = own_rows(step)
            own = pl.ds(pl.multiple_of(8 * step, 8), 8)

            def pull(q, j):
                return g[q, j, pl.ds(r - VELOCITY[q][0], 8), :]

            caches = {q: {} for q in range(Q)}
            for j in OWN:
                pop = []
                for q in range(Q):
                    _, sy, sz = VELOCITY[q]
                    if sy == 0:
                        v = pull(q, j)
                        if sz:
                            v = rolled(v, sz)
                    else:
                        cache = caches[q]
                        for k in (j, j - sy):
                            if k not in cache:
                                cache[k] = rolled(pull(q, k), sy * BS + sz)
                        if sy > 0:
                            keep = group > 0
                        else:
                            keep = group < 3
                        v = jnp.where(keep, cache[j], cache[j - sy])
                    if sz:
                        wall = z_first if sz > 0 else z_last
                        v = jnp.where(wall, g[OPPOSITE[q], j, pl.ds(r, 8), :], v)
                    f[q, j - 1, own, :] = v
                    pop.append(v)
                if with_moments:
                    store_moments(pop, j, r)

    def collide():
        @pl.loop(0, 8)
        def _(step):
            r = own_rows(step)
            own = pl.ds(pl.multiple_of(8 * step, 8), 8)
            rows = pl.ds(r, 8)
            for j in OWN:
                k = j - 1
                fluid = fl[k, own, :] > 0.0
                density = rho[k, own, :]
                a = vx[k, own, :]
                b = vy[k, own, :]
                d = uz[k, own, :]
                square = a * a + b * b + d * d
                rest = 1.25 - 1.875 * square
                big = density * (1.0 / 18.0)
                small = density * (1.0 / 36.0)
                pop0 = f[0, k, own, :]
                relaxed = density * (1.0 / 3.0) * rest - 0.25 * pop0
                g[0, j, rows, :] = jnp.where(fluid, relaxed, pop0)
                for q in range(1, Q, 2):
                    cx, cy, cz = VELOCITY[q]
                    s = None
                    for comp, val in ((cx, a), (cy, b), (cz, d)):
                        if comp:
                            if s is None:
                                s = val
                            else:
                                s = s + val if comp > 0 else s - val
                    weight = big if q < 7 else small
                    even = weight * (rest + 5.625 * (s * s))
                    odd = weight * (3.75 * s)
                    fa = f[q, k, own, :]
                    fb = f[q + 1, k, own, :]
                    g[q, j, rows, :] = jnp.where(fluid, (even + odd) - 0.25 * fa, fb)
                    g[q + 1, j, rows, :] = jnp.where(fluid, (even - odd) - 0.25 * fb, fa)

    for copy in first:
        copy.wait()

    @pl.loop(0, 8)
    def _(step):
        r = own_rows(step)
        own = pl.ds(pl.multiple_of(8 * step, 8), 8)
        for j in OWN:
            fluid = mk[j - 1, own, :] == 0
            fl[j - 1, own, :] = jnp.where(fluid, 1.0, 0.0)
            t[j, pl.ds(r, 8), :] = jnp.where(fluid, t[j, pl.ds(r, 8), :], -1.0)

    for k in range(8):
        rows = pl.ds(EDGE + 8 * k, 8)
        out = pl.ds(8 * k, 8)
        for side, tile in ((0, 1), (1, TILES)):
            sy_g[side, 0, out, :] = t[tile, rows, :]
            sy_g[side, 1, out, :] = phi[tile, rows, :]
    for j in OWN:
        to = pl.ds(j - 1, 1)
        last = EDGE + ROWS - 1
        sx_g[0, 0, to, :] = t[j, pl.ds(EDGE, 1), :]
        sx_g[0, 1, to, :] = t[j, pl.ds(EDGE + 1, 1), :]
        sx_g[0, 2, to, :] = phi[j, pl.ds(EDGE, 1), :]
        sx_g[1, 0, to, :] = t[j, pl.ds(last, 1), :]
        sx_g[1, 1, to, :] = t[j, pl.ds(last - 1, 1), :]
        sx_g[1, 2, to, :] = phi[j, pl.ds(last, 1), :]
    sx_g[:, 3:5] = jnp.zeros((2, 2, 8, LANES), jnp.float32)
    pl.semaphore_wait(barrier, N_DEV - 1)
    start(ex_g(1))

    for copy in pops:
        copy.wait()

    @pl.loop(0, 8)
    def _(step):
        r = own_rows(step)
        own = pl.ds(pl.multiple_of(8 * step, 8), 8)
        for j in OWN:
            store_moments([f[q, j - 1, own, :] for q in range(Q)], j, r)

    send_velocity(0)

    finish(ex_g(1))
    for k in range(10):
        rows = pl.ds(EDGE - 8 + 8 * k, 8)
        for side, tile in ((0, 0), (1, NT - 1)):
            t[tile, rows, :] = strip_rows(ry_g, 1, side, 0, k)
            phi[tile, rows, :] = strip_rows(ry_g, 1, side, 1, k)
    for j in OWN:
        at = pl.ds(j - 1, 1)
        last = EDGE + ROWS - 1
        t[j, pl.ds(EDGE - 1, 1), :] = rx_g[1, 0, 0, at, :]
        t[j, pl.ds(EDGE - 2, 1), :] = rx_g[1, 0, 1, at, :]
        phi[j, pl.ds(EDGE - 1, 1), :] = rx_g[1, 0, 2, at, :]
        t[j, pl.ds(last + 1, 1), :] = rx_g[1, 1, 0, at, :]
        t[j, pl.ds(last + 2, 1), :] = rx_g[1, 1, 1, at, :]
        phi[j, pl.ds(last + 1, 1), :] = rx_g[1, 1, 2, at, :]

    @pl.loop(0, 10)
    def _(step):
        r = pl.multiple_of(EDGE - 8 + 8 * step, 8)
        rows = pl.ds(r, 8)
        raw = {j: t[j, rows, :] for j in ALL}
        v = {j: jnp.maximum(raw[j], 0.0) for j in ALL}
        up = {}
        down = {}
        for j in ALL:
            fluid = jnp.where(raw[j] >= 0.0, 1.0, 0.0)
            xn = v[j] * jnp.maximum(t[j, pl.ds(r + 1, 8), :], 0.0)
            xp = v[j] * jnp.maximum(t[j, pl.ds(r - 1, 8), :], 0.0)
            yn = v[j] * y_next(v, j, up)
            yp = v[j] * y_prev(v, j, down)
            zn = jnp.where(z_last, 0.0, v[j] * rolled(v[j], -1))
            zp = jnp.where(z_first, 0.0, v[j] * rolled(v[j], 1))
            kx[j, rows, :] = xn
            ky[j, rows, :] = yn
            kym[j, rows, :] = yp
            kz[j, rows, :] = zn
            kzm[j, rows, :] = zp
            diagonal = SCREENING * fluid + (1.0 - fluid)
            dg[j, rows, :] = diagonal + xn + xp + yn + yp + zn + zp

    @pl.loop(0, 8)
    def _(step):
        r = own_rows(step)
        rows = pl.ds(r, 8)
        own = pl.ds(pl.multiple_of(8 * step, 8), 8)

        def sink(j, here_v, out):
            charge = c[0, 0, j, rows, :] - c[0, 1, j, rows, :]
            r0[j, rows, :] = fl[j - 1, own, :] * charge - out

        apply(phi, r, OWN, sink)

    send_residual(0, 0)

    def body(n, tau):
        par = lax.rem(n, 2)
        nxt = 1 - par
        take_residual(par, par)

        def to_w(r, tiles):
            def sink(j, here_v, out):
                w[j, pl.ds(r, 8), :] = out - tau * here_v

            apply(r0, r, tiles, sink)

        @pl.loop(0, 8)
        def _(step):
            to_w(own_rows(step), ALL)

        to_w(EDGE - 8, OWN)
        to_w(EDGE + ROWS, OWN)

        zero = jnp.zeros((8, LANES), jnp.float32)

        def sums(step, acc):
            r = own_rows(step)
            own = pl.ds(pl.multiple_of(8 * step, 8), 8)
            acc = list(acc)

            def sink(j, here_v, out):
                aw[j - 1, own, :] = out
                res = r0[j, pl.ds(r, 8), :]
                acc[0] = acc[0] + res * res
                acc[1] = acc[1] + res * here_v
                acc[2] = acc[2] + here_v * here_v
                acc[3] = acc[3] + here_v * out

            apply(w, r, OWN, sink)
            return tuple(acc)

        acc = lax.fori_loop(0, 8, sums, (zero,) * 4)
        rows4 = []
        for a in acc:
            a = jnp.sum(a, axis=0, keepdims=True)
            a = jnp.broadcast_to(a, (8, LANES))
            a = a + rolled(a, 2 * BS)
            rows4.append(a + rolled(a, BS))
        mine = jnp.where(
            group == 0, rows4[0],
            jnp.where(group == 1, rows4[1], jnp.where(group == 2, rows4[2], rows4[3])),
        )[0:1]
        ar[par, me] = mine
        x4, y4 = gx // 4, lax.rem(gx, 4)
        z4, core = gy // 2, lax.rem(gy, 2)
        for a, b, d, e in tile_offsets():
            dev = (
                lax.rem(x4 + a, 4) * 4 + lax.rem(y4 + b, 4),
                lax.rem(z4 + d, 4) * 2 + lax.rem(core + e, 2),
            )
            pltpu.make_async_remote_copy(
                src_ref=ar.at[par, me], dst_ref=ar.at[par, me],
                send_sem=ar_send, recv_sem=ar_recv.at[par],
                device_id=dev, device_id_type=MESH,
            ).start()

        @pl.when(n > 0)
        def _():
            take_populations(nxt)
            propagate(True)
            send_velocity(par)

        others = ar.at[par, pl.ds(0, N_DEV - 1)]
        pltpu.make_async_copy(others, others, ar_send).wait()
        pltpu.make_async_copy(others, others, ar_recv.at[par]).wait()
        parts = [ar[par, k] for k in range(8)]
        for k in range(8, N_DEV):
            parts[k % 8] = parts[k % 8] + ar[par, k]
        while len(parts) > 1:
            parts = [parts[k] + parts[k + 1] for k in range(0, len(parts), 2)]
        total = parts[0]
        where = lax.broadcasted_iota(jnp.int32, (1, LANES), 1) // BS
        s = [
            jnp.sum(jnp.where(where == k, total, 0.0), axis=1, keepdims=True) for k in range(4)
        ]
        ratio = s[1] / s[0]
        lam = tau + ratio
        first_len = 1.0 / lam
        square = first_len * first_len
        rr1 = square * (s[2] - ratio * ratio * s[0])
        beta = rr1 / s[0]
        curve = square * (
            ratio * ratio * lam * s[0] - 2.0 * ratio * (s[2] + tau * s[1]) + s[3]
        ) - beta * beta * lam * s[0]
        second_len = jnp.where(curve > 0.0, rr1 / jnp.where(curve > 0.0, curve, 1.0), 0.0)
        along_r = first_len + second_len * (first_len * ratio + beta)
        along_w = second_len * first_len
        cr = jnp.broadcast_to(along_r, (8, LANES))
        cw = jnp.broadcast_to(along_w, (8, LANES))
        keep_r = jnp.broadcast_to(1.0 - along_r * tau[0:1, 0:1], (8, LANES))

        def new_phi(r, tiles):
            rows = pl.ds(r, 8)
            for j in tiles:
                phi[j, rows, :] = phi[j, rows, :] + (cr * r0[j, rows, :] - cw * w[j, rows, :])

        @pl.loop(0, 8)
        def _(step):
            new_phi(own_rows(step), ALL)

        new_phi(EDGE - 8, OWN)
        new_phi(EDGE + ROWS, OWN)
        take_velocity(par)

        def faces(k, ca, cb, da, db, pa, pb, ua, ub, half_field):
            hu = 0.25 * (ua + ub)
            hd = 0.5 * (pb - pa)
            if half_field:
                hd = hd - half_field
            return (
                k * ((ca - cb) + (ca + cb) * (hu - hd)),
                k * ((da - db) + (da + db) * (hu + hd)),
            )

        def x_faces(j, r):
            rows = pl.ds(r, 8)
            more = pl.ds(r + 1, 8)
            p_next = phi[j, more, :]
            out = faces(
                kx[j, rows, :],
                c[par, 0, j, rows, :], c[par, 0, j, more, :],
                c[par, 1, j, rows, :], c[par, 1, j, more, :],
                phi[j, rows, :], p_next, ux[j, rows, :], ux[j, more, :], 0.5 * APPLIED,
            )
            flux[0, j - 1, rows, :] = out[0]
            flux[1, j - 1, rows, :] = out[1]
            return out, p_next

        for j in OWN:
            x_faces(j, EDGE - 8)

        @pl.loop(0, 8)
        def _(step):
            r = own_rows(step)
            rows = pl.ds(r, 8)
            less = pl.ds(r - 1, 8)
            own = pl.ds(pl.multiple_of(8 * step, 8), 8)
            p = {j: phi[j, rows, :] for j in ALL}
            a = {j: c[par, 0, j, rows, :] for j in ALL}
            b = {j: c[par, 1, j, rows, :] for j in ALL}
            v = {j: uy[j, rows, :] for j in ALL}
            pc, ac, bc, vc, pm = {}, {}, {}, {}, {}
            y0 = {}
            y1 = {}
            for j in range(NT - 1):
                pn = y_next(p, j, pc)
                y0[j], y1[j] = faces(
                    ky[j, rows, :], a[j], y_next(a, j, ac), b[j], y_next(b, j, bc),
                    p[j], pn, v[j], y_next(v, j, vc), 0.0,
                )
                if j == 0:
                    continue
                (x0, x1), p_next = x_faces(j, r)
                d0 = x0 - flux[0, j - 1, less, :]
                d1 = x1 - flux[1, j - 1, less, :]
                if j == 1:
                    y0c, y1c = {}, {}
                d0 = d0 + y0[j] - y_prev(y0, j, y0c)
                d1 = d1 + y1[j] - y_prev(y1, j, y1c)
                vz = uz[j - 1, own, :]
                z0, z1 = faces(
                    kz[j, rows, :], a[j], rolled(a[j], -1), b[j], rolled(b[j], -1),
                    p[j], rolled(p[j], -1), vz, rolled(vz, -1), 0.0,
                )
                d0 = d0 + z0 - rolled(z0, 1)
                d1 = d1 + z1 - rolled(z1, 1)
                new0 = a[j] - ION_STEP * d0
                new1 = b[j] - ION_STEP * d1
                c[nxt, 0, j, rows, :] = new0
                c[nxt, 1, j, rows, :] = new1
                charge = new0 - new1
                push = (FORCE_SCALE * RELAX_TIME) * charge * rinv[j - 1, own, :]
                vx[j - 1, own, :] = ux[j, rows, :] + push * (
                    APPLIED - 0.5 * (p_next - phi[j, less, :])
                )
                vy[j - 1, own, :] = v[j] - push * (0.5 * (pn - y_prev(p, j, pm)))
                r0[j, rows, :] = (
                    keep_r * r0[j, rows, :] - cr * w[j, rows, :] + cw * aw[j - 1, own, :]
                    + fl[j - 1, own, :] * (charge - (a[j] - b[j]))
                )

        @pl.when(n < STEPS - 1)
        def _():
            send_residual(nxt, nxt)

        collide()
        send_populations(par)
        return jnp.broadcast_to(lam, (8, LANES))

    lax.fori_loop(0, STEPS, body, jnp.ones((8, LANES), jnp.float32))

    done = []
    for b in range(2):
        for j in range(TILES):
            lanes = pl.ds(j * LANES, LANES)
            rows = pl.ds(EDGE + b * BS, BS)
            done.append((phi.at[1 + j, rows, :], pot_out.at[b, :, lanes]))
            done.append((c.at[0, :, 1 + j, rows, :], conc_out.at[:, b, :, lanes]))
    done = [pltpu.make_async_copy(s, d, out_sem.at[0, n]) for n, (s, d) in enumerate(done)]
    for copy in done:
        copy.start()
    take_populations((STEPS - 1) % 2)
    propagate(False)
    last = []
    for b in range(2):
        for j in range(TILES):
            lanes = pl.ds(j * LANES, LANES)
            last.append(
                pltpu.make_async_copy(
                    f.at[:, j, pl.ds(b * BS, BS), :],
                    pop_out.at[:, b, :, lanes],
                    out_sem.at[1, b * TILES + j],
                )
            )
    for copy in last:
        copy.start()
    for copy in done + last:
        copy.wait()


def local(populations, concentration, potential, mobility, solid_mask, block_col):
    blocks = populations.shape[1]
    anywhere = pl.BlockSpec(memory_space=pl.ANY)
    f32 = jnp.float32

    def field(*lead):
        return pltpu.VMEM(lead + (NT, NR, LANES), f32)

    def bare(*lead):
        return pltpu.VMEM(lead + (TILES, ROWS, LANES), f32)

    def vm(*shape):
        return pltpu.VMEM(shape + (LANES,), f32)

    scratch = [
        bare(Q), field(Q), field(), field(), field(), bare(), field(2, 2), field(),
        field(), field(), field(), field(), field(), field(), bare(),
        pltpu.VMEM((TILES, ROWS, LANES), jnp.int32),
        field(), field(), bare(), bare(), bare(), bare(), bare(),
        pltpu.VMEM((2, TILES, NR, LANES), f32),
        vm(2, N_DEV, 1),
        vm(2, 1, ROWS), vm(2, 2, 1, STRIP), vm(2, 4, 8), vm(2, 2, 4, 8),
        vm(2, 2, ROWS), vm(2, 2, 2, STRIP), vm(2, 5, 8), vm(2, 2, 5, 8),
        vm(2, 1, 8), vm(2, 2, 1, STRIP), vm(2, 2, 1, 8),
        pltpu.SemaphoreType.DMA((2, 64)),
        pltpu.SemaphoreType.DMA((2, 32)),
        pltpu.SemaphoreType.DMA,
        pltpu.SemaphoreType.DMA((2,)),
        pltpu.SemaphoreType.DMA((8,)), pltpu.SemaphoreType.DMA((2, 8)),
        pltpu.SemaphoreType.DMA((8,)), pltpu.SemaphoreType.DMA((2, 8)),
        pltpu.SemaphoreType.DMA((8,)), pltpu.SemaphoreType.DMA((2, 8)),
    ]
    return pl.pallas_call(
        kernel,
        out_shape=(
            jax.ShapeDtypeStruct(populations.shape, f32),
            jax.ShapeDtypeStruct(concentration.shape, f32),
            jax.ShapeDtypeStruct(potential.shape, f32),
        ),
        in_specs=[pl.BlockSpec(memory_space=pltpu.SMEM)] + [anywhere] * 5,
        out_specs=(anywhere,) * 3,
        scratch_shapes=scratch,
        compiler_params=pltpu.CompilerParams(
            collective_id=0, has_side_effects=True, vmem_limit_bytes=48 * 1024 * 1024
        ),
        cost_estimate=pl.CostEstimate(
            flops=100_000_000, bytes_accessed=12_000_000, transcendentals=0
        ),
    )(block_col, populations, concentration, potential, mobility, solid_mask)


def solution(mesh):
    split = ("gx", "gy")
    return jax.shard_map(
        local,
        mesh=mesh,
        in_specs=(
            P(None, split, None, None),
            P(None, split, None, None),
            P(split, None, None),
            P(split, None, None),
            P(split, None, None),
            P(),
        ),
        out_specs=(P(None, split, None, None), P(None, split, None, None), P(split, None, None)),
        check_vma=False,
    )
```

```python
import jax
import jax.numpy as jnp
from jax import lax
from jax.experimental import pallas as pl
from jax.experimental.pallas import tpu as pltpu
from jax.sharding import PartitionSpec as P

BS = 32
Q = 19
STEPS = 4
N_GX = 16
N_GY = 8
N_DEV = N_GX * N_GY
VELOCITY = (
    (0, 0, 0),
    (1, 0, 0),
    (-1, 0, 0),
    (0, 1, 0),
    (0, -1, 0),
    (0, 0, 1),
    (0, 0, -1),
    (1, 1, 0),
    (-1, -1, 0),
    (1, -1, 0),
    (-1, 1, 0),
    (1, 0, 1),
    (-1, 0, -1),
    (1, 0, -1),
    (-1, 0, 1),
    (0, 1, 1),
    (0, -1, -1),
    (0, 1, -1),
    (0, -1, 1),
)
OPPOSITE = (0, 2, 1, 4, 3, 6, 5, 8, 7, 10, 9, 12, 11, 14, 13, 16, 15, 18, 17)
UP_Y = (3, 7, 10, 15, 17)
DOWN_Y = (4, 8, 9, 16, 18)
UP_X = (1, 7, 9, 11, 13)
DOWN_X = (2, 8, 10, 12, 14)
RELAX_TIME = 0.8
SCREENING = 0.5
APPLIED = 0.4
ION_STEP = 0.05
FORCE_SCALE = 0.5

MESH = pl.DeviceIdType.MESH
LANES = 128
TILES = 8
ROWS = 64
EDGE = 16
NR = ROWS + 2 * EDGE
NT = TILES + 2
VMEM_LIMIT = 60 * 1024 * 1024
UNROLL_APPLY = 4
UNROLL_XFLUX = 1
UNROLL_BORDER = 2
UNROLL_INSIDE = 2
UNROLL_LBM = 2
SIDE = 40
STRIP = ROWS + 2 * SIDE


def tile_offsets():
    hops = lambda a: min(a, 4 - a)
    offs = [
        (a, b, c, d)
        for a in range(4)
        for b in range(4)
        for c in range(4)
        for d in range(2)
        if a + b + c + d
    ]
    offs.sort(key=lambda o: -(hops(o[0]) + hops(o[1]) + hops(o[2]) + 0.1 * o[3]))
    return offs


def stream(g, f, r, own, tiles, sink):
    lane = lax.broadcasted_iota(jnp.int32, (8, LANES), 1)
    depth = lane % BS
    group = lane // BS

    def pull(q, j):
        return g[q, j, pl.ds(r - VELOCITY[q][0], 8), :]

    caches = {q: {} for q in range(Q)}
    for j in tiles:
        pop = []
        for q in range(Q):
            _, sy, sz = VELOCITY[q]
            if sy == 0:
                v = pull(q, j)
                if sz:
                    v = pltpu.roll(v, sz % LANES, 1)
            else:
                cache = caches[q]
                for k in (j, j - sy):
                    if k not in cache:
                        cache[k] = pltpu.roll(pull(q, k), (sy * BS + sz) % LANES, 1)
                v = jnp.where(group > 0 if sy > 0 else group < 3, cache[j], cache[j - sy])
            if sz:
                wall = depth == (0 if sz > 0 else BS - 1)
                v = jnp.where(wall, g[OPPOSITE[q], j, pl.ds(r, 8), :], v)
            f[q, own, (j - 1) * LANES : j * LANES] = v
            pop.append(v)
        if sink is not None:
            sink(pop, j)


def kernel(
    col_ref, pop_hbm, conc_hbm, pot_hbm, mob_hbm, mask_hbm,
    g_out, conc_out, pot_out,
    f, g, phi, r0, w, aw, c0, c1, n0, n1, t, kx, ky, kym, kz, kzm, dg, fl, mk,
    ux, uy, uz, rho, rinv, vx, vy, flux0, flux1, dy0, dy1, dz0, dz1, slope, r_next,
    ar, sy_r, ry_r, sx_r, rx_r, sy_g, ry_g, sx_g, rx_g, sx_u, ry_u, rx_u, sy_i, ry_i, sx_i, rx_i,
    in_sem, out_sem, ar_send, ar_recv, send_r, recv_r, send_g, recv_g, send_u, recv_u,
    send_i, recv_i,
):
    gx = lax.axis_index("gx")
    gy = lax.axis_index("gy")
    right = lax.rem(gx + 1, N_GX)
    left = lax.rem(gx + N_GX - 1, N_GX)
    above = lax.rem(gy + 1, N_GY)
    below = lax.rem(gy + N_GY - 1, N_GY)
    me = gx * N_GY + gy

    lane = lax.broadcasted_iota(jnp.int32, (8, LANES), 1)
    depth = lane % BS
    group = lane // BS
    z_first = depth == 0
    z_last = depth == BS - 1

    loads = []
    for j in range(TILES):
        lanes = pl.ds(j * LANES, LANES)
        rows = pl.ds(EDGE, ROWS)
        loads.append((mob_hbm.at[:, lanes], t.at[1 + j, rows, :]))
        loads.append((mask_hbm.at[:, lanes], mk.at[j]))
        loads.append((pot_hbm.at[:, lanes], phi.at[1 + j, rows, :]))
        loads.append((conc_hbm.at[0, :, lanes], c0.at[1 + j, rows, :]))
        loads.append((conc_hbm.at[1, :, lanes], c1.at[1 + j, rows, :]))
    first = [pltpu.make_async_copy(s, d, in_sem.at[n]) for n, (s, d) in enumerate(loads)]
    pops = [pltpu.make_async_copy(pop_hbm, f, in_sem.at[len(first)])]
    for copy in first:
        copy.start()
    for copy in pops:
        copy.start()

    barrier = pltpu.get_barrier_semaphore()

    def greet(k, _):
        other = lax.rem(me + k, N_DEV)
        pl.semaphore_signal(
            barrier, inc=1, device_id=(other // N_GY, lax.rem(other, N_GY)), device_id_type=MESH
        )
        return 0

    lax.fori_loop(1, N_DEV, greet, 0)

    def exchange(par, strip_src, strip_dst, x_src, x_dst, send, recv):
        copies = []
        for to_y, dst_side in ((below, 1), (above, 0)):
            src_side = 1 - dst_side
            for to_x, src_row, dst_row, count in (
                (gx, 0, SIDE, ROWS),
                (right, ROWS - SIDE, 0, SIDE),
                (left, 0, SIDE + ROWS, SIDE),
            ):
                copies.append(
                    (
                        strip_src(src_side, src_row, count),
                        strip_dst.at[par, dst_side, :, pl.ds(dst_row, count), :],
                        (to_x, to_y),
                    )
                )
        copies.append((x_src.at[1], x_dst.at[par, 0], (right, gy)))
        copies.append((x_src.at[0], x_dst.at[par, 1], (left, gy)))
        return [
            pltpu.make_async_remote_copy(
                src_ref=s, dst_ref=d, send_sem=send.at[k], recv_sem=recv.at[par, k],
                device_id=dev, device_id_type=MESH,
            )
            for k, (s, d, dev) in enumerate(copies)
        ]

    def staged(ref):
        return lambda side, row, count: ref.at[side, :, pl.ds(row, count), :]

    def ex_r(par):
        return exchange(par, staged(sy_r), ry_r, sx_r, rx_r, send_r, recv_r)

    def ex_g(par):
        return exchange(par, staged(sy_g), ry_g, sx_g, rx_g, send_g, recv_g)

    def ex_u(par):
        def src(side, row, count):
            tile = TILES if side == 1 else 1
            return uy.at[pl.ds(tile, 1), pl.ds(EDGE + row, count), :]

        return exchange(par, src, ry_u, sx_u, rx_u, send_u, recv_u)

    def start(copies):
        for copy in copies:
            copy.start()

    def finish(copies):
        for copy in copies:
            copy.wait()

    here = col_ref[2 * gy]
    ahead = [
        jnp.broadcast_to(here - col_ref[2 * other], (8, LANES)) for other in (below, above)
    ]
    less = [v < 0 for v in ahead]
    more = [v > 0 for v in ahead]

    def strip_rows(ref, par, side, number, k):
        first, same, last = [
            ref[par, side, number, pl.ds(start + 8 * k, 8), :] for start in (0, BS, 2 * BS)
        ]
        return jnp.where(less[side], first, jnp.where(more[side], last, same))

    def own_rows(step):
        return pl.multiple_of(EDGE + 8 * step, 8)

    def rolled(v, shift):
        return pltpu.roll(v, shift % LANES, 1)

    def y_next(load, tile, cache, top=NT - 1):
        for k in (tile, min(tile + 1, top)):
            if k not in cache:
                cache[k] = rolled(load(k), -BS)
        if tile == top:
            return cache[tile]
        return jnp.where(group < 3, cache[tile], cache[tile + 1])

    def y_prev(load, tile, cache, bottom=0):
        for k in (max(tile - 1, bottom), tile):
            if k not in cache:
                cache[k] = rolled(load(k), BS)
        if tile == bottom:
            return cache[tile]
        return jnp.where(group > 0, cache[tile], cache[tile - 1])

    def loader(ref, rows):
        return lambda j: ref[j, rows, :]

    def apply(ref, r, tiles, sink):
        rows = pl.ds(r, 8)
        load = loader(ref, rows)
        up = {}
        down = {}
        for j in tiles:
            here_v = load(j)
            out = dg[j, rows, :] * here_v
            out = out - kx[j, rows, :] * ref[j, pl.ds(r + 1, 8), :]
            out = out - kx[j, pl.ds(r - 1, 8), :] * ref[j, pl.ds(r - 1, 8), :]
            out = out - ky[j, rows, :] * y_next(load, j, up)
            out = out - kym[j, rows, :] * y_prev(load, j, down)
            out = out - kz[j, rows, :] * rolled(here_v, -1)
            out = out - kzm[j, rows, :] * rolled(here_v, 1)
            sink(j, here_v, out)

    OWN = list(range(1, TILES + 1))
    ALL = list(range(NT))

    def border(work):
        @pl.loop(0, 2, unroll=True)
        def _(k):
            work(7 * k, OWN)

        @pl.loop(1, 7, unroll=UNROLL_BORDER)
        def _(step):
            work(step, OWN[:1])
            work(step, OWN[-1:])

    def inside(work):
        @pl.loop(1, 7, unroll=UNROLL_INSIDE)
        def _(step):
            work(step, OWN[1:-1])

    def moments(pop):
        p = pop
        xp = p[7] + p[9] + p[11] + p[13] + p[1]
        xm = p[8] + p[10] + p[12] + p[14] + p[2]
        yp = p[15] + p[17] + p[3]
        ym = p[16] + p[18] + p[4]
        density = p[0] + xp + xm + yp + ym + (p[5] + p[6])
        jx = xp - xm
        jy = (yp - ym) + ((p[7] + p[10]) - (p[8] + p[9]))
        jz = (p[5] - p[6]) + ((p[11] + p[14]) - (p[12] + p[13])) + (
            (p[15] + p[18]) - (p[16] + p[17])
        )
        inverse = 1.0 / density
        return density, inverse, jx * inverse, jy * inverse, jz * inverse

    def store_moments(pop, j, r):
        density, inverse, a, b, d = moments(pop)
        rows = pl.ds(r, 8)
        own = pl.ds(pl.multiple_of(r - EDGE, 8), 8)
        rho[j - 1, own, :] = density
        rinv[j - 1, own, :] = inverse
        ux[j, rows, :] = a
        uy[j, rows, :] = b
        uz[j - 1, own, :] = d

    def send_velocity(par):
        for j in OWN:
            sx_u[0, 0, pl.ds(j - 1, 1), :] = ux[j, pl.ds(EDGE, 1), :]
            sx_u[1, 0, pl.ds(j - 1, 1), :] = ux[j, pl.ds(EDGE + ROWS - 1, 1), :]
        start(ex_u(par))

    def take_velocity(par):
        finish(ex_u(par))
        for j in OWN:
            ux[j, pl.ds(EDGE - 1, 1), :] = rx_u[par, 0, 0, pl.ds(j - 1, 1), :]
            ux[j, pl.ds(EDGE + ROWS, 1), :] = rx_u[par, 1, 0, pl.ds(j - 1, 1), :]
        for k in range(10):
            rows = pl.ds(EDGE - 8 + 8 * k, 8)
            uy[0, rows, :] = strip_rows(ry_u, par, 0, 0, k)
            uy[NT - 1, rows, :] = strip_rows(ry_u, par, 1, 0, k)

    def send_residual(par):
        for k in range(8):
            out = pl.ds(8 * k, 8)
            a = rolled(n0[0, out, :], 2 * BS)
            b = rolled(n1[0, out, :], 3 * BS)
            sy_r[0, 0, out, :] = jnp.where(
                group < 2, r_next[0, out, :], jnp.where(group == 2, a, b)
            )
            a = rolled(n0[TILES - 1, out, :], BS)
            b = rolled(n1[TILES - 1, out, :], 2 * BS)
            sy_r[1, 0, out, :] = jnp.where(
                group > 1, r_next[TILES - 1, out, :], jnp.where(group == 0, a, b)
            )
        for k in range(TILES):
            to = pl.ds(k, 1)
            for side, row, ahead in ((0, 0, 1), (1, ROWS - 1, -1)):
                sx_r[side, 0, to, :] = r_next[k, pl.ds(row, 1), :]
                sx_r[side, 1, to, :] = r_next[k, pl.ds(row + ahead, 1), :]
                sx_r[side, 2, to, :] = n0[k, pl.ds(row, 1), :]
                sx_r[side, 3, to, :] = n1[k, pl.ds(row, 1), :]
        start(ex_r(par))

    def take_residual(par):
        finish(ex_r(par))
        for k in range(10):
            rows = pl.ds(EDGE - 8 + 8 * k, 8)
            v = strip_rows(ry_r, par, 0, 0, k)
            r0[0, rows, :] = v
            c0[0, rows, :] = rolled(v, 3 * BS)
            c1[0, rows, :] = rolled(v, 2 * BS)
            v = strip_rows(ry_r, par, 1, 0, k)
            r0[NT - 1, rows, :] = v
            c0[NT - 1, rows, :] = rolled(v, 2 * BS)
            c1[NT - 1, rows, :] = rolled(v, BS)
        for j in OWN:
            at = pl.ds(j - 1, 1)
            last = EDGE + ROWS - 1
            r0[j, pl.ds(EDGE - 1, 1), :] = rx_r[par, 0, 0, at, :]
            r0[j, pl.ds(EDGE - 2, 1), :] = rx_r[par, 0, 1, at, :]
            r0[j, pl.ds(last + 1, 1), :] = rx_r[par, 1, 0, at, :]
            r0[j, pl.ds(last + 2, 1), :] = rx_r[par, 1, 1, at, :]
            for s, ref in enumerate((c0, c1)):
                ref[j, pl.ds(EDGE - 1, 1), :] = rx_r[par, 0, 2 + s, at, :]
                ref[j, pl.ds(last + 1, 1), :] = rx_r[par, 1, 2 + s, at, :]

    def send_populations(par):
        for side, tile, names in ((0, 1, DOWN_Y), (1, TILES, UP_Y)):
            home = 0 if side == 0 else 3
            for k in range(8):
                rows = pl.ds(EDGE + 8 * k, 8)
                out = pl.ds(8 * k, 8)
                parts = [
                    rolled(g[q, tile, rows, :], (at % 4 - home) * BS)
                    for at, q in enumerate(names)
                ]
                sy_g[side, 0, out, :] = jnp.where(
                    group == 0, parts[0],
                    jnp.where(group == 1, parts[1], jnp.where(group == 2, parts[2], parts[3])),
                )
                sy_g[side, 1, out, :] = parts[4]
        for side, row, names in ((0, EDGE, DOWN_X), (1, EDGE + ROWS - 1, UP_X)):
            for at, q in enumerate(names):
                for j in OWN:
                    sx_g[side, at, pl.ds(j - 1, 1), :] = g[q, j, pl.ds(row, 1), :]
        start(ex_g(par))

    def take_populations(par):
        finish(ex_g(par))
        for side, tile, names in ((0, 0, UP_Y), (1, NT - 1, DOWN_Y)):
            home = 3 if side == 0 else 0
            for k in range(10):
                rows = pl.ds(EDGE - 8 + 8 * k, 8)
                v = strip_rows(ry_g, par, side, 0, k)
                for at, q in enumerate(names):
                    if at == 4:
                        v = strip_rows(ry_g, par, side, 1, k)
                    g[q, tile, rows, :] = rolled(v, (home - at % 4) * BS)
        for side, row, names in ((0, EDGE - 1, UP_X), (1, EDGE + ROWS, DOWN_X)):
            for at, q in enumerate(names):
                for j in OWN:
                    g[q, j, pl.ds(row, 1), :] = rx_g[par, side, at, pl.ds(j - 1, 1), :]

    def propagate(step, tiles):
        r = own_rows(step)
        own = pl.ds(pl.multiple_of(8 * step, 8), 8)
        stream(g, f, r, own, tiles, lambda pop, j: store_moments(pop, j, r))

    def collide():
        @pl.loop(0, 8, unroll=UNROLL_LBM)
        def _(step):
            r = own_rows(step)
            own = pl.ds(pl.multiple_of(8 * step, 8), 8)
            rows = pl.ds(r, 8)
            for j in OWN:
                k = j - 1
                c0[j, rows, :] = n0[k, own, :]
                c1[j, rows, :] = n1[k, own, :]
                r0[j, rows, :] = r_next[k, own, :]
                fluid = fl[k, own, :] > 0.0
                density = rho[k, own, :]
                a = vx[k, own, :]
                b = vy[k, own, :]
                d = uz[k, own, :]
                square = a * a + b * b + d * d
                rest = 1.25 - 1.875 * square
                big = density * (1.0 / 18.0)
                small = density * (1.0 / 36.0)
                lanes = slice(k * LANES, j * LANES)
                pop0 = f[0, own, lanes]
                relaxed = density * (1.0 / 3.0) * rest - 0.25 * pop0
                g[0, j, rows, :] = jnp.where(fluid, relaxed, pop0)
                for q in range(1, Q, 2):
                    cx, cy, cz = VELOCITY[q]
                    s = None
                    for comp, val in ((cx, a), (cy, b), (cz, d)):
                        if comp:
                            if s is None:
                                s = val
                            else:
                                s = s + val if comp > 0 else s - val
                    weight = big if q < 7 else small
                    even = weight * (rest + 5.625 * (s * s))
                    odd = weight * (3.75 * s)
                    fa = f[q, own, lanes]
                    fb = f[q + 1, own, lanes]
                    g[q, j, rows, :] = jnp.where(fluid, (even + odd) - 0.25 * fa, fb)
                    g[q + 1, j, rows, :] = jnp.where(fluid, (even - odd) - 0.25 * fb, fa)

    for copy in first:
        copy.wait()

    @pl.loop(0, 8)
    def _(step):
        r = own_rows(step)
        own = pl.ds(pl.multiple_of(8 * step, 8), 8)
        for j in OWN:
            fluid = mk[j - 1, own, :] == 0
            fl[j - 1, own, :] = jnp.where(fluid, 1.0, 0.0)
            t[j, pl.ds(r, 8), :] = jnp.where(fluid, t[j, pl.ds(r, 8), :], -1.0)

    starts = (t, phi, c0, c1)
    depths = (3, 3, 2, 2)
    for j in OWN:
        at = 0
        for ref, deep in zip(starts, depths):
            for layer in range(deep):
                to = pl.ds(j - 1, 1)
                sx_i[0, at, to, :] = ref[j, pl.ds(EDGE + layer, 1), :]
                sx_i[1, at, to, :] = ref[j, pl.ds(EDGE + ROWS - 1 - layer, 1), :]
                at += 1
    for n, ref in enumerate(starts):
        for k in range(8):
            rows = pl.ds(EDGE + 8 * k, 8)
            sy_i[0, n, pl.ds(8 * k, 8), :] = ref[1, rows, :]
            sy_i[1, n, pl.ds(8 * k, 8), :] = ref[TILES, rows, :]
    first_halo = exchange(0, staged(sy_i), ry_i, sx_i, rx_i, send_i, recv_i)
    pl.semaphore_wait(barrier, N_DEV - 1)
    start(first_halo)

    for copy in pops:
        copy.wait()

    @pl.loop(0, 8)
    def _(step):
        r = own_rows(step)
        own = pl.ds(pl.multiple_of(8 * step, 8), 8)
        for j in OWN:
            store_moments(
                [f[q, own, (j - 1) * LANES : j * LANES] for q in range(Q)], j, r
            )

    send_velocity(0)

    finish(first_halo)
    for k in range(10):
        rows = pl.ds(EDGE - 8 + 8 * k, 8)
        for n, ref in enumerate(starts):
            ref[0, rows, :] = strip_rows(ry_i, 0, 0, n, k)
            ref[NT - 1, rows, :] = strip_rows(ry_i, 0, 1, n, k)
    for j in OWN:
        at = 0
        for ref, deep in zip(starts, depths):
            for layer in range(deep):
                of = pl.ds(j - 1, 1)
                ref[j, pl.ds(EDGE - 1 - layer, 1), :] = rx_i[0, 0, at, of, :]
                ref[j, pl.ds(EDGE + ROWS + layer, 1), :] = rx_i[0, 1, at, of, :]
                at += 1

    @pl.loop(0, 10)
    def _(step):
        r = pl.multiple_of(EDGE - 8 + 8 * step, 8)
        rows = pl.ds(r, 8)
        raw = {j: t[j, rows, :] for j in ALL}
        v = {j: jnp.maximum(raw[j], 0.0) for j in ALL}
        up = {}
        down = {}
        for j in ALL:
            fluid = jnp.where(raw[j] >= 0.0, 1.0, 0.0)
            xn = v[j] * jnp.maximum(t[j, pl.ds(r + 1, 8), :], 0.0)
            xp = v[j] * jnp.maximum(t[j, pl.ds(r - 1, 8), :], 0.0)
            yn = v[j] * y_next(v.get, j, up)
            yp = v[j] * y_prev(v.get, j, down)
            zn = jnp.where(z_last, 0.0, v[j] * rolled(v[j], -1))
            zp = jnp.where(z_first, 0.0, v[j] * rolled(v[j], 1))
            kx[j, rows, :] = xn
            ky[j, rows, :] = yn
            kym[j, rows, :] = yp
            kz[j, rows, :] = zn
            kzm[j, rows, :] = zp
            diagonal = SCREENING * fluid + (1.0 - fluid)
            dg[j, rows, :] = diagonal + xn + xp + yn + yp + zn + zp

    @pl.loop(0, 10)
    def _(step):
        r = pl.multiple_of(EDGE - 8 + 8 * step, 8)
        rows = pl.ds(r, 8)

        def sink(j, here_v, out):
            charge = c0[j, rows, :] - c1[j, rows, :]
            r0[j, rows, :] = jnp.where(t[j, rows, :] >= 0.0, charge, 0.0) - out

        apply(phi, r, ALL, sink)

    def body(n, tau):
        par = lax.rem(n, 2)
        nxt = 1 - par
        @pl.when(n > 0)
        def _():
            take_residual(par)


        def to_w(r, tiles):
            def sink(j, here_v, out):
                w[j, pl.ds(r, 8), :] = out - tau * here_v

            apply(r0, r, tiles, sink)

        @pl.loop(0, 8, unroll=UNROLL_APPLY)
        def _(step):
            to_w(own_rows(step), ALL)

        to_w(EDGE - 8, OWN)
        to_w(EDGE + ROWS, OWN)

        zero = jnp.zeros((8, LANES), jnp.float32)

        def sums(step, acc):
            r = own_rows(step)
            own = pl.ds(pl.multiple_of(8 * step, 8), 8)
            acc = list(acc)

            def sink(j, here_v, out):
                aw[j - 1, own, :] = out
                res = r0[j, pl.ds(r, 8), :]
                acc[0] = acc[0] + res * res
                acc[1] = acc[1] + res * here_v
                acc[2] = acc[2] + here_v * here_v
                acc[3] = acc[3] + here_v * out

            apply(w, r, OWN, sink)
            return tuple(acc)

        acc = lax.fori_loop(0, 8, sums, (zero,) * 4, unroll=UNROLL_APPLY)
        rows4 = []
        for a in acc:
            a = jnp.sum(a, axis=0, keepdims=True)
            a = jnp.broadcast_to(a, (8, LANES))
            a = a + rolled(a, 2 * BS)
            rows4.append(a + rolled(a, BS))
        mine = jnp.where(
            group == 0, rows4[0],
            jnp.where(group == 1, rows4[1], jnp.where(group == 2, rows4[2], rows4[3])),
        )[0:1]
        ar[par, me] = mine
        x4, y4 = gx // 4, lax.rem(gx, 4)
        z4, core = gy // 2, lax.rem(gy, 2)
        for a, b, d, e in tile_offsets():
            dev = (
                lax.rem(x4 + a, 4) * 4 + lax.rem(y4 + b, 4),
                lax.rem(z4 + d, 4) * 2 + lax.rem(core + e, 2),
            )
            pltpu.make_async_remote_copy(
                src_ref=ar.at[par, me], dst_ref=ar.at[par, me],
                send_sem=ar_send, recv_sem=ar_recv.at[par],
                device_id=dev, device_id_type=MESH,
            ).start()

        @pl.when(n > 0)
        def _():
            take_populations(nxt)
            border(propagate)
            send_velocity(par)
            inside(propagate)

        others = ar.at[par, pl.ds(0, N_DEV - 1)]
        pltpu.make_async_copy(others, others, ar_send).wait()
        pltpu.make_async_copy(others, others, ar_recv.at[par]).wait()
        parts = [ar[par, k] for k in range(8)]
        for k in range(8, N_DEV):
            parts[k % 8] = parts[k % 8] + ar[par, k]
        while len(parts) > 1:
            parts = [parts[k] + parts[k + 1] for k in range(0, len(parts), 2)]
        total = parts[0]
        where = lax.broadcasted_iota(jnp.int32, (1, LANES), 1) // BS
        s = [
            jnp.sum(jnp.where(where == k, total, 0.0), axis=1, keepdims=True) for k in range(4)
        ]
        ratio = s[1] / s[0]
        lam = tau + ratio
        first_len = 1.0 / lam
        square = first_len * first_len
        rr1 = square * (s[2] - ratio * ratio * s[0])
        beta = rr1 / s[0]
        curve = square * (
            ratio * ratio * lam * s[0] - 2.0 * ratio * (s[2] + tau * s[1]) + s[3]
        ) - beta * beta * lam * s[0]
        second_len = jnp.where(curve > 0.0, rr1 / jnp.where(curve > 0.0, curve, 1.0), 0.0)
        along_r = first_len + second_len * (first_len * ratio + beta)
        along_w = second_len * first_len
        cr = jnp.broadcast_to(along_r, (8, LANES))
        cw = jnp.broadcast_to(along_w, (8, LANES))
        keep_r = jnp.broadcast_to(1.0 - along_r * tau[0:1, 0:1], (8, LANES))

        def new_phi(r, tiles):
            rows = pl.ds(r, 8)
            new = [
                phi[j, rows, :] + (cr * r0[j, rows, :] - cw * w[j, rows, :]) for j in tiles
            ]
            for j, v in zip(tiles, new):
                phi[j, rows, :] = v

        @pl.loop(0, 8, unroll=UNROLL_APPLY)
        def _(step):
            new_phi(own_rows(step), ALL)

        new_phi(EDGE - 8, OWN)
        new_phi(EDGE + ROWS, OWN)
        take_velocity(par)

        def faces(k, ca, cb, da, db, pa, pb, ua, ub, half_field):
            hu = 0.25 * (ua + ub)
            hd = 0.5 * (pb - pa)
            if half_field:
                hd = hd - half_field
            return (
                k * ((ca - cb) + (ca + cb) * (hu - hd)),
                k * ((da - db) + (da + db) * (hu + hd)),
            )

        def x_faces(j, r):
            rows = pl.ds(r, 8)
            more = pl.ds(r + 1, 8)
            out = faces(
                kx[j, rows, :],
                c0[j, rows, :], c0[j, more, :], c1[j, rows, :], c1[j, more, :],
                phi[j, rows, :], phi[j, more, :], ux[j, rows, :], ux[j, more, :], 0.5 * APPLIED,
            )
            flux0[j - 1, rows, :] = out[0]
            flux1[j - 1, rows, :] = out[1]

        @pl.loop(0, 9, unroll=UNROLL_XFLUX)
        def _(step):
            for j in OWN:
                x_faces(j, pl.multiple_of(EDGE - 8 + 8 * step, 8))

        def y_faces(step, tiles):
            r = own_rows(step)
            rows = pl.ds(r, 8)
            own = pl.ds(pl.multiple_of(8 * step, 8), 8)
            p, a, b, v = [loader(ref, rows) for ref in (phi, c0, c1, uy)]
            caches = [{} for _ in range(8)]
            for j in tiles:
                pn, an, bn, vn = [y_next(ld, j, ca) for ld, ca in zip((p, a, b, v), caches)]
                pp, ap, bp, vp = [y_prev(ld, j, ca) for ld, ca in zip((p, a, b, v), caches[4:])]
                pj, aj, bj, vj = p(j), a(j), b(j), v(j)
                f0, f1 = faces(ky[j, rows, :], aj, an, bj, bn, pj, pn, vj, vn, 0.0)
                g0, g1 = faces(kym[j, rows, :], ap, aj, bp, bj, pp, pj, vp, vj, 0.0)
                dy0[j - 1, own, :] = f0 - g0
                dy1[j - 1, own, :] = f1 - g1
                slope[j - 1, own, :] = pn - pp

        def z_faces(step, tiles):
            rows = pl.ds(own_rows(step), 8)
            own = pl.ds(pl.multiple_of(8 * step, 8), 8)
            for j in tiles:
                here_v = (c0[j, rows, :], c1[j, rows, :], phi[j, rows, :], uz[j - 1, own, :])
                aj, bj, pj, vj = here_v
                an, bn, pn, vn = [rolled(v, -1) for v in here_v]
                ap, bp, pp, vp = [rolled(v, 1) for v in here_v]
                f0, f1 = faces(kz[j, rows, :], aj, an, bj, bn, pj, pn, vj, vn, 0.0)
                g0, g1 = faces(kzm[j, rows, :], ap, aj, bp, bj, pp, pj, vp, vj, 0.0)
                dz0[j - 1, own, :] = f0 - g0
                dz1[j - 1, own, :] = f1 - g1

        def transport_step(step, tiles):
            r = own_rows(step)
            rows = pl.ds(r, 8)
            less = pl.ds(r - 1, 8)
            own = pl.ds(pl.multiple_of(8 * step, 8), 8)
            for j in tiles:
                k = j - 1
                d0 = flux0[k, rows, :] - flux0[k, less, :] + dy0[k, own, :] + dz0[k, own, :]
                d1 = flux1[k, rows, :] - flux1[k, less, :] + dy1[k, own, :] + dz1[k, own, :]
                aj = c0[j, rows, :]
                bj = c1[j, rows, :]
                new0 = aj - ION_STEP * d0
                new1 = bj - ION_STEP * d1
                n0[k, own, :] = new0
                n1[k, own, :] = new1
                charge = new0 - new1
                push = (FORCE_SCALE * RELAX_TIME) * charge * rinv[k, own, :]
                vx[k, own, :] = ux[j, rows, :] + push * (
                    APPLIED - 0.5 * (phi[j, pl.ds(r + 1, 8), :] - phi[j, less, :])
                )
                vy[k, own, :] = uy[j, rows, :] - push * (0.5 * slope[k, own, :])
                r_next[k, own, :] = (
                    keep_r * r0[j, rows, :] - cr * w[j, rows, :] + cw * aw[k, own, :]
                    + fl[k, own, :] * (charge - (aj - bj))
                )

        border(y_faces)
        border(z_faces)
        border(transport_step)

        @pl.when(n < STEPS - 1)
        def _():
            send_residual(nxt)

        inside(y_faces)
        inside(z_faces)
        inside(transport_step)
        collide()
        send_populations(par)
        return jnp.broadcast_to(lam, (8, LANES))

    lax.fori_loop(0, STEPS, body, jnp.ones((8, LANES), jnp.float32))

    own = pl.ds(EDGE, ROWS)
    out = [(g.at[:, pl.ds(1, TILES), own, :], g_out.at[:, pl.ds(1, TILES), own, :])]
    for j in range(TILES):
        lanes = pl.ds(j * LANES, LANES)
        out.append((phi.at[1 + j, own, :], pot_out.at[:, lanes]))
        out.append((c0.at[1 + j, own, :], conc_out.at[0, :, lanes]))
        out.append((c1.at[1 + j, own, :], conc_out.at[1, :, lanes]))
    done = [pltpu.make_async_copy(s, d, out_sem.at[n]) for n, (s, d) in enumerate(out)]
    start(done)
    take_populations((STEPS - 1) % 2)
    rims = [
        pltpu.make_async_copy(g.at[part], g_out.at[part], out_sem.at[len(done) + n])
        for n, part in enumerate(ghost_parts())
    ]
    start(rims)
    finish(done + rims)


def ghost_parts():
    parts = [(q, pl.ds(0, 1), pl.ds(EDGE - 8, ROWS + 16)) for q in UP_Y]
    parts += [(q, pl.ds(NT - 1, 1), pl.ds(EDGE - 8, ROWS + 16)) for q in DOWN_Y]
    parts += [(q, pl.ds(1, TILES), pl.ds(EDGE - 8, 8)) for q in UP_X]
    parts += [(q, pl.ds(1, TILES), pl.ds(EDGE + ROWS, 8)) for q in DOWN_X]
    return parts


def last_kernel(
    g_hbm, conc_hbm, pot_hbm, pop_out, conc_out, pot_out, g, f, conc, pot, in_sem, out_sem
):
    rims = [
        pltpu.make_async_copy(g_hbm.at[part], g.at[part], in_sem.at[4 + n])
        for n, part in enumerate(ghost_parts())
    ]
    chunks = []
    for n, (low, high) in enumerate(((16, 40), (40, 56), (56, 72), (72, 80))):
        part = (slice(None), pl.ds(1, TILES), pl.ds(low, high - low))
        chunks.append(pltpu.make_async_copy(g_hbm.at[part], g.at[part], in_sem.at[n]))
    chunks[0].start()
    for copy in rims:
        copy.start()
    for copy in chunks[1:]:
        copy.start()
    small = [
        pltpu.make_async_copy(conc_hbm, conc, in_sem.at[24]),
        pltpu.make_async_copy(pot_hbm, pot, in_sem.at[25]),
    ]
    for copy in small:
        copy.start()
    others = [
        pltpu.make_async_copy(conc, conc_out, out_sem.at[4]),
        pltpu.make_async_copy(pot, pot_out, out_sem.at[5]),
    ]
    for copy in rims:
        copy.wait()
    outs = []
    for n in range(4):
        chunks[n].wait()
        for step in (2 * n, 2 * n + 1):
            stream(g, f, EDGE + 8 * step, pl.ds(8 * step, 8), range(1, TILES + 1), None)
        part = (slice(None), pl.ds(16 * n, 16))
        outs.append(pltpu.make_async_copy(f.at[part], pop_out.at[part], out_sem.at[n]))
        outs[-1].start()
        if n == 0:
            for copy in small:
                copy.wait()
            for copy in others:
                copy.start()
    for copy in outs + others:
        copy.wait()


def local(populations, concentration, potential, mobility, solid_mask, block_col):
    anywhere = pl.BlockSpec(memory_space=pl.ANY)
    f32 = jnp.float32

    def field(*lead):
        return pltpu.VMEM(lead + (NT, NR, LANES), f32)

    def bare(*lead):
        return pltpu.VMEM(lead + (TILES, ROWS, LANES), f32)

    def vm(*shape):
        return pltpu.VMEM(shape + (LANES,), f32)

    scratch = [
        pltpu.VMEM((Q, ROWS, TILES * LANES), f32), field(Q),
        field(), field(), field(), bare(), field(), field(), bare(), bare(), field(),
        field(), field(), field(), field(), field(), field(), bare(),
        pltpu.VMEM((TILES, ROWS, LANES), jnp.int32),
        field(), field(), bare(), bare(), bare(), bare(), bare(),
        vm(TILES, NR), vm(TILES, NR), bare(), bare(), bare(), bare(), bare(), bare(),
        vm(2, N_DEV, 1),
        vm(2, 1, ROWS), vm(2, 2, 1, STRIP), vm(2, 4, 8), vm(2, 2, 4, 8),
        vm(2, 2, ROWS), vm(2, 2, 2, STRIP), vm(2, 5, 8), vm(2, 2, 5, 8),
        vm(2, 1, 8), vm(2, 2, 1, STRIP), vm(2, 2, 1, 8),
        vm(2, 4, ROWS), vm(1, 2, 4, STRIP), vm(2, 10, 8), vm(1, 2, 10, 8),
        pltpu.SemaphoreType.DMA((48,)),
        pltpu.SemaphoreType.DMA((48,)),
        pltpu.SemaphoreType.DMA,
        pltpu.SemaphoreType.DMA((2,)),
        pltpu.SemaphoreType.DMA((8,)), pltpu.SemaphoreType.DMA((2, 8)),
        pltpu.SemaphoreType.DMA((8,)), pltpu.SemaphoreType.DMA((2, 8)),
        pltpu.SemaphoreType.DMA((8,)), pltpu.SemaphoreType.DMA((2, 8)),
        pltpu.SemaphoreType.DMA((8,)), pltpu.SemaphoreType.DMA((1, 8)),
    ]
    flat = (ROWS, TILES * LANES)
    g_last, conc, pot = pl.pallas_call(
        kernel,
        out_shape=(
            jax.ShapeDtypeStruct((Q, NT, NR, LANES), f32),
            jax.ShapeDtypeStruct((2,) + flat, f32),
            jax.ShapeDtypeStruct(flat, f32),
        ),
        in_specs=[pl.BlockSpec(memory_space=pltpu.SMEM)] + [anywhere] * 5,
        out_specs=(anywhere,) * 3,
        scratch_shapes=scratch,
        compiler_params=pltpu.CompilerParams(
            collective_id=0, has_side_effects=True, vmem_limit_bytes=VMEM_LIMIT
        ),
        cost_estimate=pl.CostEstimate(
            flops=100_000_000, bytes_accessed=12_000_000, transcendentals=0
        ),
    )(
        block_col,
        populations.reshape((Q,) + flat),
        concentration.reshape((2,) + flat),
        potential.reshape(flat),
        mobility.reshape(flat),
        solid_mask.reshape(flat),
    )
    pop, conc, pot = pl.pallas_call(
        last_kernel,
        out_shape=(
            jax.ShapeDtypeStruct((Q,) + flat, f32),
            jax.ShapeDtypeStruct((2,) + flat, f32),
            jax.ShapeDtypeStruct(flat, f32),
        ),
        in_specs=[anywhere] * 3,
        out_specs=(anywhere,) * 3,
        scratch_shapes=[
            pltpu.VMEM((Q, NT, NR, LANES), f32),
            pltpu.VMEM((Q,) + flat, f32),
            pltpu.VMEM((2,) + flat, f32),
            pltpu.VMEM(flat, f32),
            pltpu.SemaphoreType.DMA((26,)),
            pltpu.SemaphoreType.DMA((6,)),
        ],
        compiler_params=pltpu.CompilerParams(vmem_limit_bytes=VMEM_LIMIT),
        cost_estimate=pl.CostEstimate(
            flops=10_000_000, bytes_accessed=12_000_000, transcendentals=0
        ),
    )(g_last, conc, pot)
    return (
        pop.reshape(populations.shape),
        conc.reshape(concentration.shape),
        pot.reshape(potential.shape),
    )


def solution(mesh):
    split = ("gx", "gy")
    return jax.shard_map(
        local,
        mesh=mesh,
        in_specs=(
            P(None, split, None, None),
            P(None, split, None, None),
            P(split, None, None),
            P(split, None, None),
            P(split, None, None),
            P(),
        ),
        out_specs=(P(None, split, None, None), P(None, split, None, None), P(split, None, None)),
        check_vma=False,
    )
```

```python
import jax
import jax.numpy as jnp
from jax import lax
from jax.experimental import pallas as pl
from jax.experimental.pallas import tpu as pltpu
from jax.sharding import PartitionSpec as P

BS = 32
Q = 19
STEPS = 4
N_GX = 16
N_GY = 8
N_DEV = N_GX * N_GY
VELOCITY = (
    (0, 0, 0),
    (1, 0, 0),
    (-1, 0, 0),
    (0, 1, 0),
    (0, -1, 0),
    (0, 0, 1),
    (0, 0, -1),
    (1, 1, 0),
    (-1, -1, 0),
    (1, -1, 0),
    (-1, 1, 0),
    (1, 0, 1),
    (-1, 0, -1),
    (1, 0, -1),
    (-1, 0, 1),
    (0, 1, 1),
    (0, -1, -1),
    (0, 1, -1),
    (0, -1, 1),
)
OPPOSITE = (0, 2, 1, 4, 3, 6, 5, 8, 7, 10, 9, 12, 11, 14, 13, 16, 15, 18, 17)
UP_Y = (3, 7, 10, 15, 17)
DOWN_Y = (4, 8, 9, 16, 18)
UP_X = (1, 7, 9, 11, 13)
DOWN_X = (2, 8, 10, 12, 14)
RELAX_TIME = 0.8
SCREENING = 0.5
APPLIED = 0.4
ION_STEP = 0.05
FORCE_SCALE = 0.5

MESH = pl.DeviceIdType.MESH
LANES = 128
TILES = 8
ROWS = 64
EDGE = 16
NR = ROWS + 2 * EDGE
NT = TILES + 2
VMEM_LIMIT = 60 * 1024 * 1024
UNROLL_APPLY = 4
UNROLL_BORDER = 3
UNROLL_INSIDE = 2
UNROLL_LBM = 2
SIDE = 40
STRIP = ROWS + 2 * SIDE


def tile_offsets():
    hops = lambda a: min(a, 4 - a)
    offs = [
        (a, b, c, d)
        for a in range(4)
        for b in range(4)
        for c in range(4)
        for d in range(2)
        if a + b + c + d
    ]
    offs.sort(key=lambda o: -(hops(o[0]) + hops(o[1]) + hops(o[2]) + 0.1 * o[3]))
    return offs


def stream(g, f, r, own, tiles, sink):
    lane = lax.broadcasted_iota(jnp.int32, (8, LANES), 1)
    depth = lane % BS
    group = lane // BS

    def pull(q, j):
        return g[q, j, pl.ds(r - VELOCITY[q][0], 8), :]

    caches = {q: {} for q in range(Q)}
    for j in tiles:
        pop = []
        for q in range(Q):
            _, sy, sz = VELOCITY[q]
            if sy == 0:
                v = pull(q, j)
                if sz:
                    v = pltpu.roll(v, sz % LANES, 1)
            else:
                cache = caches[q]
                for k in (j, j - sy):
                    if k not in cache:
                        cache[k] = pltpu.roll(pull(q, k), (sy * BS + sz) % LANES, 1)
                v = jnp.where(group > 0 if sy > 0 else group < 3, cache[j], cache[j - sy])
            if sz:
                wall = depth == (0 if sz > 0 else BS - 1)
                v = jnp.where(wall, g[OPPOSITE[q], j, pl.ds(r, 8), :], v)
            f[q, own, (j - 1) * LANES : j * LANES] = v
            pop.append(v)
        if sink is not None:
            sink(pop, j)


def kernel(
    col_ref, pop_hbm, conc_hbm, pot_hbm, mob_hbm, mask_hbm,
    g_out, conc_out, pot_out,
    f, g, phi, r0, w, aw, c0, c1, n0, n1, t, kx, ky, kym, kz, kzm, dg, fl, mk,
    ux, uy, uz, rho, rinv, vx, vy, dy0, dy1, dz0, dz1, slope, r_next,
    ar, sy_r, ry_r, sx_r, rx_r, sy_g, ry_g, sx_g, rx_g, sx_u, ry_u, rx_u, sy_i, ry_i, sx_i, rx_i,
    in_sem, out_sem, ar_send, ar_recv, send_r, recv_r, send_g, recv_g, send_u, recv_u,
    send_i, recv_i,
):
    gx = lax.axis_index("gx")
    gy = lax.axis_index("gy")
    right = lax.rem(gx + 1, N_GX)
    left = lax.rem(gx + N_GX - 1, N_GX)
    above = lax.rem(gy + 1, N_GY)
    below = lax.rem(gy + N_GY - 1, N_GY)
    me = gx * N_GY + gy

    lane = lax.broadcasted_iota(jnp.int32, (8, LANES), 1)
    depth = lane % BS
    group = lane // BS
    z_first = depth == 0
    z_last = depth == BS - 1

    x4, y4 = gx // 4, lax.rem(gx, 4)
    z4, core = gy // 2, lax.rem(gy, 2)
    to_gx = {
        (a, b): lax.rem(x4 + a, 4) * 4 + lax.rem(y4 + b, 4) for a in range(4) for b in range(4)
    }
    to_gy = {
        (d, e): lax.rem(z4 + d, 4) * 2 + lax.rem(core + e, 2) for d in range(4) for e in range(2)
    }

    loads = []
    for j in range(TILES):
        lanes = pl.ds(j * LANES, LANES)
        rows = pl.ds(EDGE, ROWS)
        loads.append((mob_hbm.at[:, lanes], t.at[1 + j, rows, :]))
        loads.append((mask_hbm.at[:, lanes], mk.at[j]))
        loads.append((pot_hbm.at[:, lanes], phi.at[1 + j, rows, :]))
        loads.append((conc_hbm.at[0, :, lanes], c0.at[1 + j, rows, :]))
        loads.append((conc_hbm.at[1, :, lanes], c1.at[1 + j, rows, :]))
    first = [pltpu.make_async_copy(s, d, in_sem.at[n]) for n, (s, d) in enumerate(loads)]
    pops = [pltpu.make_async_copy(pop_hbm, f, in_sem.at[len(first)])]
    for copy in first:
        copy.start()
    for copy in pops:
        copy.start()

    barrier = pltpu.get_barrier_semaphore()

    def greet(k, _):
        other = lax.rem(me + k, N_DEV)
        pl.semaphore_signal(
            barrier, inc=1, device_id=(other // N_GY, lax.rem(other, N_GY)), device_id_type=MESH
        )
        return 0

    lax.fori_loop(1, N_DEV, greet, 0)

    def exchange(par, strip_src, strip_dst, x_src, x_dst, send, recv):
        copies = []
        for to_y, dst_side in ((below, 1), (above, 0)):
            src_side = 1 - dst_side
            for to_x, src_row, dst_row, count in (
                (gx, 0, SIDE, ROWS),
                (right, ROWS - SIDE, 0, SIDE),
                (left, 0, SIDE + ROWS, SIDE),
            ):
                copies.append(
                    (
                        strip_src(src_side, src_row, count),
                        strip_dst.at[par, dst_side, :, pl.ds(dst_row, count), :],
                        (to_x, to_y),
                    )
                )
        copies.append((x_src.at[1], x_dst.at[par, 0], (right, gy)))
        copies.append((x_src.at[0], x_dst.at[par, 1], (left, gy)))
        return [
            pltpu.make_async_remote_copy(
                src_ref=s, dst_ref=d, send_sem=send.at[k], recv_sem=recv.at[par, k],
                device_id=dev, device_id_type=MESH,
            )
            for k, (s, d, dev) in enumerate(copies)
        ]

    def staged(ref):
        return lambda side, row, count: ref.at[side, :, pl.ds(row, count), :]

    def ex_r(par):
        return exchange(par, staged(sy_r), ry_r, sx_r, rx_r, send_r, recv_r)

    def ex_g(par):
        return exchange(par, staged(sy_g), ry_g, sx_g, rx_g, send_g, recv_g)

    def ex_u(par):
        def src(side, row, count):
            tile = TILES if side == 1 else 1
            return uy.at[pl.ds(tile, 1), pl.ds(EDGE + row, count), :]

        return exchange(par, src, ry_u, sx_u, rx_u, send_u, recv_u)

    def start(copies):
        for copy in copies:
            copy.start()

    def finish(copies):
        for copy in copies:
            copy.wait()

    here = col_ref[2 * gy]
    ahead = [
        jnp.broadcast_to(here - col_ref[2 * other], (8, LANES)) for other in (below, above)
    ]
    less = [v < 0 for v in ahead]
    more = [v > 0 for v in ahead]

    def strip_rows(ref, par, side, number, k):
        first, same, last = [
            ref[par, side, number, pl.ds(start + 8 * k, 8), :] for start in (0, BS, 2 * BS)
        ]
        return jnp.where(less[side], first, jnp.where(more[side], last, same))

    def own_rows(step):
        return pl.multiple_of(EDGE + 8 * step, 8)

    def rolled(v, shift):
        return pltpu.roll(v, shift % LANES, 1)

    def y_next(load, tile, cache, top=NT - 1):
        for k in (tile, min(tile + 1, top)):
            if k not in cache:
                cache[k] = rolled(load(k), -BS)
        if tile == top:
            return cache[tile]
        return jnp.where(group < 3, cache[tile], cache[tile + 1])

    def y_prev(load, tile, cache, bottom=0):
        for k in (max(tile - 1, bottom), tile):
            if k not in cache:
                cache[k] = rolled(load(k), BS)
        if tile == bottom:
            return cache[tile]
        return jnp.where(group > 0, cache[tile], cache[tile - 1])

    def loader(ref, rows):
        return lambda j: ref[j, rows, :]

    def apply(ref, r, tiles, sink):
        rows = pl.ds(r, 8)
        load = loader(ref, rows)
        up = {}
        down = {}
        for j in tiles:
            here_v = load(j)
            out = dg[j, rows, :] * here_v
            out = out - kx[j, rows, :] * ref[j, pl.ds(r + 1, 8), :]
            out = out - kx[j, pl.ds(r - 1, 8), :] * ref[j, pl.ds(r - 1, 8), :]
            out = out - ky[j, rows, :] * y_next(load, j, up)
            out = out - kym[j, rows, :] * y_prev(load, j, down)
            out = out - kz[j, rows, :] * rolled(here_v, -1)
            out = out - kzm[j, rows, :] * rolled(here_v, 1)
            sink(j, here_v, out)

    OWN = list(range(1, TILES + 1))
    ALL = list(range(NT))

    def border(work):
        @pl.loop(0, 2, unroll=True)
        def _(k):
            work(7 * k, OWN)

        @pl.loop(1, 7, unroll=UNROLL_BORDER)
        def _(step):
            work(step, OWN[:1])
            work(step, OWN[-1:])

    def inside(work):
        @pl.loop(1, 7, unroll=UNROLL_INSIDE)
        def _(step):
            work(step, OWN[1:-1])

    def rim(work):
        @pl.loop(0, 2, unroll=True)
        def _(k):
            work(7 * k, ALL)

        @pl.loop(1, 7, unroll=UNROLL_BORDER)
        def _(step):
            work(step, ALL[:2])
            work(step, ALL[-2:])

    def rows_beyond(work, tiles=OWN):
        @pl.loop(0, 2, unroll=True)
        def _(k):
            work(9 * k - 1, tiles)

    def to_w(tau):
        def work(step, tiles):
            r = own_rows(step)

            def sink(j, here_v, out):
                w[j, pl.ds(r, 8), :] = out - tau * here_v

            apply(r0, r, tiles, sink)

        return work

    def moments(pop):
        p = pop
        xp = p[7] + p[9] + p[11] + p[13] + p[1]
        xm = p[8] + p[10] + p[12] + p[14] + p[2]
        yp = p[15] + p[17] + p[3]
        ym = p[16] + p[18] + p[4]
        density = p[0] + xp + xm + yp + ym + (p[5] + p[6])
        jx = xp - xm
        jy = (yp - ym) + ((p[7] + p[10]) - (p[8] + p[9]))
        jz = (p[5] - p[6]) + ((p[11] + p[14]) - (p[12] + p[13])) + (
            (p[15] + p[18]) - (p[16] + p[17])
        )
        inverse = 1.0 / density
        return density, inverse, jx * inverse, jy * inverse, jz * inverse

    def store_moments(pop, j, r):
        density, inverse, a, b, d = moments(pop)
        rows = pl.ds(r, 8)
        own = pl.ds(pl.multiple_of(r - EDGE, 8), 8)
        rho[j - 1, own, :] = density
        rinv[j - 1, own, :] = inverse
        ux[j, rows, :] = a
        uy[j, rows, :] = b
        uz[j - 1, own, :] = d

    def send_velocity(par):
        for j in OWN:
            sx_u[0, 0, pl.ds(j - 1, 1), :] = ux[j, pl.ds(EDGE, 1), :]
            sx_u[1, 0, pl.ds(j - 1, 1), :] = ux[j, pl.ds(EDGE + ROWS - 1, 1), :]
        start(ex_u(par))

    def take_velocity(par):
        finish(ex_u(par))
        for j in OWN:
            ux[j, pl.ds(EDGE - 1, 1), :] = rx_u[par, 0, 0, pl.ds(j - 1, 1), :]
            ux[j, pl.ds(EDGE + ROWS, 1), :] = rx_u[par, 1, 0, pl.ds(j - 1, 1), :]
        for k in range(10):
            rows = pl.ds(EDGE - 8 + 8 * k, 8)
            uy[0, rows, :] = strip_rows(ry_u, par, 0, 0, k)
            uy[NT - 1, rows, :] = strip_rows(ry_u, par, 1, 0, k)

    def send_residual(par):
        for k in range(8):
            out = pl.ds(8 * k, 8)
            a = rolled(n0[0, out, :], 2 * BS)
            b = rolled(n1[0, out, :], 3 * BS)
            sy_r[0, 0, out, :] = jnp.where(
                group < 2, r_next[0, out, :], jnp.where(group == 2, a, b)
            )
            a = rolled(n0[TILES - 1, out, :], BS)
            b = rolled(n1[TILES - 1, out, :], 2 * BS)
            sy_r[1, 0, out, :] = jnp.where(
                group > 1, r_next[TILES - 1, out, :], jnp.where(group == 0, a, b)
            )
        for k in range(TILES):
            to = pl.ds(k, 1)
            for side, row, ahead in ((0, 0, 1), (1, ROWS - 1, -1)):
                sx_r[side, 0, to, :] = r_next[k, pl.ds(row, 1), :]
                sx_r[side, 1, to, :] = r_next[k, pl.ds(row + ahead, 1), :]
                sx_r[side, 2, to, :] = n0[k, pl.ds(row, 1), :]
                sx_r[side, 3, to, :] = n1[k, pl.ds(row, 1), :]
        start(ex_r(par))

    def take_residual(par):
        finish(ex_r(par))
        for k in range(10):
            rows = pl.ds(EDGE - 8 + 8 * k, 8)
            v = strip_rows(ry_r, par, 0, 0, k)
            r0[0, rows, :] = v
            c0[0, rows, :] = rolled(v, 3 * BS)
            c1[0, rows, :] = rolled(v, 2 * BS)
            v = strip_rows(ry_r, par, 1, 0, k)
            r0[NT - 1, rows, :] = v
            c0[NT - 1, rows, :] = rolled(v, 2 * BS)
            c1[NT - 1, rows, :] = rolled(v, BS)
        for j in OWN:
            at = pl.ds(j - 1, 1)
            last = EDGE + ROWS - 1
            r0[j, pl.ds(EDGE - 1, 1), :] = rx_r[par, 0, 0, at, :]
            r0[j, pl.ds(EDGE - 2, 1), :] = rx_r[par, 0, 1, at, :]
            r0[j, pl.ds(last + 1, 1), :] = rx_r[par, 1, 0, at, :]
            r0[j, pl.ds(last + 2, 1), :] = rx_r[par, 1, 1, at, :]
            for s, ref in enumerate((c0, c1)):
                ref[j, pl.ds(EDGE - 1, 1), :] = rx_r[par, 0, 2 + s, at, :]
                ref[j, pl.ds(last + 1, 1), :] = rx_r[par, 1, 2 + s, at, :]

    def send_populations(par):
        for side, tile, names in ((0, 1, DOWN_Y), (1, TILES, UP_Y)):
            home = 0 if side == 0 else 3
            for k in range(8):
                rows = pl.ds(EDGE + 8 * k, 8)
                out = pl.ds(8 * k, 8)
                parts = [
                    rolled(g[q, tile, rows, :], (at % 4 - home) * BS)
                    for at, q in enumerate(names)
                ]
                sy_g[side, 0, out, :] = jnp.where(
                    group == 0, parts[0],
                    jnp.where(group == 1, parts[1], jnp.where(group == 2, parts[2], parts[3])),
                )
                sy_g[side, 1, out, :] = parts[4]
        for side, row, names in ((0, EDGE, DOWN_X), (1, EDGE + ROWS - 1, UP_X)):
            for at, q in enumerate(names):
                for j in OWN:
                    sx_g[side, at, pl.ds(j - 1, 1), :] = g[q, j, pl.ds(row, 1), :]
        start(ex_g(par))

    def take_populations(par):
        finish(ex_g(par))
        for side, tile, names in ((0, 0, UP_Y), (1, NT - 1, DOWN_Y)):
            home = 3 if side == 0 else 0
            for k in range(10):
                rows = pl.ds(EDGE - 8 + 8 * k, 8)
                v = strip_rows(ry_g, par, side, 0, k)
                for at, q in enumerate(names):
                    if at == 4:
                        v = strip_rows(ry_g, par, side, 1, k)
                    g[q, tile, rows, :] = rolled(v, (home - at % 4) * BS)
        for side, row, names in ((0, EDGE - 1, UP_X), (1, EDGE + ROWS, DOWN_X)):
            for at, q in enumerate(names):
                for j in OWN:
                    g[q, j, pl.ds(row, 1), :] = rx_g[par, side, at, pl.ds(j - 1, 1), :]

    def propagate(step, tiles):
        r = own_rows(step)
        own = pl.ds(pl.multiple_of(8 * step, 8), 8)
        stream(g, f, r, own, tiles, lambda pop, j: store_moments(pop, j, r))

    def collide(step, tiles):
        r = own_rows(step)
        own = pl.ds(pl.multiple_of(8 * step, 8), 8)
        rows = pl.ds(r, 8)
        for j in tiles:
            k = j - 1
            fluid = fl[k, own, :] > 0.0
            density = rho[k, own, :]
            a = vx[k, own, :]
            b = vy[k, own, :]
            d = uz[k, own, :]
            square = a * a + b * b + d * d
            rest = 1.25 - 1.875 * square
            big = density * (1.0 / 18.0)
            small = density * (1.0 / 36.0)
            lanes = slice(k * LANES, j * LANES)
            pop0 = f[0, own, lanes]
            relaxed = density * (1.0 / 3.0) * rest - 0.25 * pop0
            g[0, j, rows, :] = jnp.where(fluid, relaxed, pop0)
            for q in range(1, Q, 2):
                cx, cy, cz = VELOCITY[q]
                s = None
                for comp, val in ((cx, a), (cy, b), (cz, d)):
                    if comp:
                        if s is None:
                            s = val
                        else:
                            s = s + val if comp > 0 else s - val
                weight = big if q < 7 else small
                even = weight * (rest + 5.625 * (s * s))
                odd = weight * (3.75 * s)
                fa = f[q, own, lanes]
                fb = f[q + 1, own, lanes]
                g[q, j, rows, :] = jnp.where(fluid, (even + odd) - 0.25 * fa, fb)
                g[q + 1, j, rows, :] = jnp.where(fluid, (even - odd) - 0.25 * fb, fa)

    for copy in first:
        copy.wait()

    @pl.loop(0, 8)
    def _(step):
        r = own_rows(step)
        own = pl.ds(pl.multiple_of(8 * step, 8), 8)
        for j in OWN:
            fluid = mk[j - 1, own, :] == 0
            fl[j - 1, own, :] = jnp.where(fluid, 1.0, 0.0)
            t[j, pl.ds(r, 8), :] = jnp.where(fluid, t[j, pl.ds(r, 8), :], -1.0)

    starts = (t, phi, c0, c1)
    depths = (3, 3, 2, 2)
    for j in OWN:
        at = 0
        for ref, deep in zip(starts, depths):
            for layer in range(deep):
                to = pl.ds(j - 1, 1)
                sx_i[0, at, to, :] = ref[j, pl.ds(EDGE + layer, 1), :]
                sx_i[1, at, to, :] = ref[j, pl.ds(EDGE + ROWS - 1 - layer, 1), :]
                at += 1
    for n, ref in enumerate(starts):
        for k in range(8):
            rows = pl.ds(EDGE + 8 * k, 8)
            sy_i[0, n, pl.ds(8 * k, 8), :] = ref[1, rows, :]
            sy_i[1, n, pl.ds(8 * k, 8), :] = ref[TILES, rows, :]
    first_halo = exchange(0, staged(sy_i), ry_i, sx_i, rx_i, send_i, recv_i)
    pl.semaphore_wait(barrier, N_DEV - 1)
    start(first_halo)

    def coefficients(step, tiles):
        r = own_rows(step)
        rows = pl.ds(r, 8)

        def load(j):
            return jnp.maximum(t[j, rows, :], 0.0)

        up = {}
        down = {}
        for j in tiles:
            raw = t[j, rows, :]
            v = load(j)
            fluid = jnp.where(raw >= 0.0, 1.0, 0.0)
            xn = v * jnp.maximum(t[j, pl.ds(r + 1, 8), :], 0.0)
            xp = v * jnp.maximum(t[j, pl.ds(r - 1, 8), :], 0.0)
            yn = v * y_next(load, j, up)
            yp = v * y_prev(load, j, down)
            zn = jnp.where(z_last, 0.0, v * rolled(v, -1))
            zp = jnp.where(z_first, 0.0, v * rolled(v, 1))
            kx[j, rows, :] = xn
            ky[j, rows, :] = yn
            kym[j, rows, :] = yp
            kz[j, rows, :] = zn
            kzm[j, rows, :] = zp
            diagonal = SCREENING * fluid + (1.0 - fluid)
            dg[j, rows, :] = diagonal + xn + xp + yn + yp + zn + zp

    def first_residual(step, tiles):
        r = own_rows(step)
        rows = pl.ds(r, 8)

        def sink(j, here_v, out):
            charge = c0[j, rows, :] - c1[j, rows, :]
            r0[j, rows, :] = jnp.where(t[j, rows, :] >= 0.0, charge, 0.0) - out

        apply(phi, r, tiles, sink)

    inside(coefficients)
    for copy in pops:
        copy.wait()

    @pl.loop(0, 8)
    def _(step):
        r = own_rows(step)
        own = pl.ds(pl.multiple_of(8 * step, 8), 8)
        for j in OWN:
            store_moments(
                [f[q, own, (j - 1) * LANES : j * LANES] for q in range(Q)], j, r
            )

    send_velocity(0)

    finish(first_halo)
    for k in range(10):
        rows = pl.ds(EDGE - 8 + 8 * k, 8)
        for n, ref in enumerate(starts):
            ref[0, rows, :] = strip_rows(ry_i, 0, 0, n, k)
            ref[NT - 1, rows, :] = strip_rows(ry_i, 0, 1, n, k)
    for j in OWN:
        at = 0
        for ref, deep in zip(starts, depths):
            for layer in range(deep):
                of = pl.ds(j - 1, 1)
                ref[j, pl.ds(EDGE - 1 - layer, 1), :] = rx_i[0, 0, at, of, :]
                ref[j, pl.ds(EDGE + ROWS + layer, 1), :] = rx_i[0, 1, at, of, :]
                at += 1

    rim(coefficients)
    rows_beyond(coefficients, ALL)
    rim(first_residual)
    rows_beyond(first_residual, ALL)
    inside(first_residual)

    def body(n, tau):
        par = lax.rem(n, 2)
        nxt = 1 - par
        @pl.when(n > 0)
        def _():
            take_residual(par)


        make_w = to_w(tau)
        rim(make_w)
        rows_beyond(make_w)

        zero = jnp.zeros((8, LANES), jnp.float32)

        def sums(step, acc):
            r = own_rows(step)
            own = pl.ds(pl.multiple_of(8 * step, 8), 8)
            acc = list(acc)

            def sink(j, here_v, out):
                aw[j - 1, own, :] = out
                res = r0[j, pl.ds(r, 8), :]
                acc[0] = acc[0] + res * res
                acc[1] = acc[1] + res * here_v
                acc[2] = acc[2] + here_v * here_v
                acc[3] = acc[3] + here_v * out

            apply(w, r, OWN, sink)
            return tuple(acc)

        acc = lax.fori_loop(0, 8, sums, (zero,) * 4, unroll=UNROLL_APPLY)
        rows4 = []
        for a in acc:
            a = jnp.sum(a, axis=0, keepdims=True)
            a = jnp.broadcast_to(a, (8, LANES))
            a = a + rolled(a, 2 * BS)
            rows4.append(a + rolled(a, BS))
        mine = jnp.where(
            group == 0, rows4[0],
            jnp.where(group == 1, rows4[1], jnp.where(group == 2, rows4[2], rows4[3])),
        )[0:1]
        ar[par, me] = mine
        for a, b, d, e in tile_offsets():
            dev = (to_gx[a, b], to_gy[d, e])
            pltpu.make_async_remote_copy(
                src_ref=ar.at[par, me], dst_ref=ar.at[par, me],
                send_sem=ar_send, recv_sem=ar_recv.at[par],
                device_id=dev, device_id_type=MESH,
            ).start()

        @pl.when(n > 0)
        def _():
            take_populations(nxt)
            border(propagate)
            send_velocity(par)
            inside(propagate)

        others = ar.at[par, pl.ds(0, N_DEV - 1)]
        pltpu.make_async_copy(others, others, ar_send).wait()
        pltpu.make_async_copy(others, others, ar_recv.at[par]).wait()
        parts = [ar[par, k] for k in range(8)]
        for k in range(8, N_DEV):
            parts[k % 8] = parts[k % 8] + ar[par, k]
        while len(parts) > 1:
            parts = [parts[k] + parts[k + 1] for k in range(0, len(parts), 2)]
        total = parts[0]
        where = lax.broadcasted_iota(jnp.int32, (1, LANES), 1) // BS
        s = [
            jnp.sum(jnp.where(where == k, total, 0.0), axis=1, keepdims=True) for k in range(4)
        ]
        ratio = s[1] / s[0]
        lam = tau[0:1, 0:1] + ratio
        first_len = 1.0 / lam
        square = first_len * first_len
        rr1 = square * (s[2] - ratio * ratio * s[0])
        beta = rr1 / s[0]
        curve = square * (
            ratio * ratio * lam * s[0] - 2.0 * ratio * (s[2] + tau[0:1, 0:1] * s[1]) + s[3]
        ) - beta * beta * lam * s[0]
        lam_all = jnp.broadcast_to(lam, (8, LANES))
        second_len = jnp.where(curve > 0.0, rr1 / jnp.where(curve > 0.0, curve, 1.0), 0.0)
        along_r = first_len + second_len * (first_len * ratio + beta)
        along_w = second_len * first_len
        cr = jnp.broadcast_to(along_r, (8, LANES))
        cw = jnp.broadcast_to(along_w, (8, LANES))
        keep_r = jnp.broadcast_to(1.0 - along_r * tau[0:1, 0:1], (8, LANES))

        def new_phi(r, tiles):
            rows = pl.ds(r, 8)
            new = [
                phi[j, rows, :] + (cr * r0[j, rows, :] - cw * w[j, rows, :]) for j in tiles
            ]
            for j, v in zip(tiles, new):
                phi[j, rows, :] = v

        @pl.loop(0, 8, unroll=UNROLL_APPLY)
        def _(step):
            new_phi(own_rows(step), ALL)

        new_phi(EDGE - 8, OWN)
        new_phi(EDGE + ROWS, OWN)
        take_velocity(par)

        def faces(k, ca, cb, da, db, pa, pb, ua, ub, half_field):
            hu = 0.25 * (ua + ub)
            hd = 0.5 * (pb - pa)
            if half_field:
                hd = hd - half_field
            return (
                k * ((ca - cb) + (ca + cb) * (hu - hd)),
                k * ((da - db) + (da + db) * (hu + hd)),
            )

        def y_faces(step, tiles):
            r = own_rows(step)
            rows = pl.ds(r, 8)
            own = pl.ds(pl.multiple_of(8 * step, 8), 8)
            p, a, b, v = [loader(ref, rows) for ref in (phi, c0, c1, uy)]
            caches = [{} for _ in range(8)]
            for j in tiles:
                pn, an, bn, vn = [y_next(ld, j, ca) for ld, ca in zip((p, a, b, v), caches)]
                pp, ap, bp, vp = [y_prev(ld, j, ca) for ld, ca in zip((p, a, b, v), caches[4:])]
                pj, aj, bj, vj = p(j), a(j), b(j), v(j)
                f0, f1 = faces(ky[j, rows, :], aj, an, bj, bn, pj, pn, vj, vn, 0.0)
                g0, g1 = faces(kym[j, rows, :], ap, aj, bp, bj, pp, pj, vp, vj, 0.0)
                dy0[j - 1, own, :] = f0 - g0
                dy1[j - 1, own, :] = f1 - g1
                slope[j - 1, own, :] = pn - pp

        def z_faces(step, tiles):
            rows = pl.ds(own_rows(step), 8)
            own = pl.ds(pl.multiple_of(8 * step, 8), 8)
            for j in tiles:
                here_v = (c0[j, rows, :], c1[j, rows, :], phi[j, rows, :], uz[j - 1, own, :])
                aj, bj, pj, vj = here_v
                an, bn, pn, vn = [rolled(v, -1) for v in here_v]
                ap, bp, pp, vp = [rolled(v, 1) for v in here_v]
                f0, f1 = faces(kz[j, rows, :], aj, an, bj, bn, pj, pn, vj, vn, 0.0)
                g0, g1 = faces(kzm[j, rows, :], ap, aj, bp, bj, pp, pj, vp, vj, 0.0)
                dz0[j - 1, own, :] = f0 - g0
                dz1[j - 1, own, :] = f1 - g1

        def transport_step(step, tiles):
            r = own_rows(step)
            rows = pl.ds(r, 8)
            less = pl.ds(r - 1, 8)
            more = pl.ds(r + 1, 8)
            own = pl.ds(pl.multiple_of(8 * step, 8), 8)
            for j in tiles:
                k = j - 1
                aj, bj, pj, vj = [ref[j, rows, :] for ref in (c0, c1, phi, ux)]
                an, bn, pn, vn = [ref[j, more, :] for ref in (c0, c1, phi, ux)]
                ap, bp, pp, vp = [ref[j, less, :] for ref in (c0, c1, phi, ux)]
                half = 0.5 * APPLIED
                f0, f1 = faces(kx[j, rows, :], aj, an, bj, bn, pj, pn, vj, vn, half)
                g0, g1 = faces(kx[j, less, :], ap, aj, bp, bj, pp, pj, vp, vj, half)
                d0 = f0 - g0 + dy0[k, own, :] + dz0[k, own, :]
                d1 = f1 - g1 + dy1[k, own, :] + dz1[k, own, :]
                new0 = aj - ION_STEP * d0
                new1 = bj - ION_STEP * d1
                n0[k, own, :] = new0
                n1[k, own, :] = new1
                charge = new0 - new1
                push = (FORCE_SCALE * RELAX_TIME) * charge * rinv[k, own, :]
                vx[k, own, :] = vj + push * (APPLIED - 0.5 * (pn - pp))
                vy[k, own, :] = uy[j, rows, :] - push * (0.5 * slope[k, own, :])
                r_next[k, own, :] = (
                    keep_r * r0[j, rows, :] - cr * w[j, rows, :] + cw * aw[k, own, :]
                    + fl[k, own, :] * (charge - (aj - bj))
                )

        border(y_faces)
        border(z_faces)
        border(transport_step)

        @pl.when(n < STEPS - 1)
        def _():
            send_residual(nxt)

        border(collide)
        send_populations(par)
        inside(y_faces)
        inside(z_faces)
        inside(transport_step)
        inside(collide)

        @pl.loop(0, 8, unroll=2)
        def _(step):
            rows = pl.ds(own_rows(step), 8)
            own = pl.ds(pl.multiple_of(8 * step, 8), 8)
            for j in OWN:
                c0[j, rows, :] = n0[j - 1, own, :]
                c1[j, rows, :] = n1[j - 1, own, :]
                r0[j, rows, :] = r_next[j - 1, own, :]

        inside(to_w(lam_all))
        return lam_all

    one = jnp.ones((8, LANES), jnp.float32)
    inside(to_w(one))
    lax.fori_loop(0, STEPS, body, one)

    own = pl.ds(EDGE, ROWS)
    out = [(g.at[:, pl.ds(1, TILES), own, :], g_out.at[:, pl.ds(1, TILES), own, :])]
    for j in range(TILES):
        lanes = pl.ds(j * LANES, LANES)
        out.append((phi.at[1 + j, own, :], pot_out.at[:, lanes]))
        out.append((c0.at[1 + j, own, :], conc_out.at[0, :, lanes]))
        out.append((c1.at[1 + j, own, :], conc_out.at[1, :, lanes]))
    done = [pltpu.make_async_copy(s, d, out_sem.at[n]) for n, (s, d) in enumerate(out)]
    start(done)
    take_populations((STEPS - 1) % 2)
    rims = [
        pltpu.make_async_copy(g.at[part], g_out.at[part], out_sem.at[len(done) + n])
        for n, part in enumerate(ghost_parts())
    ]
    start(rims)
    finish(done + rims)


def ghost_parts():
    parts = [(q, pl.ds(0, 1), pl.ds(EDGE - 8, ROWS + 16)) for q in UP_Y]
    parts += [(q, pl.ds(NT - 1, 1), pl.ds(EDGE - 8, ROWS + 16)) for q in DOWN_Y]
    parts += [(q, pl.ds(1, TILES), pl.ds(EDGE - 8, 8)) for q in UP_X]
    parts += [(q, pl.ds(1, TILES), pl.ds(EDGE + ROWS, 8)) for q in DOWN_X]
    return parts


def last_kernel(
    g_hbm, conc_hbm, pot_hbm, pop_out, conc_out, pot_out, g, f, conc, pot, in_sem, out_sem
):
    rims = [
        pltpu.make_async_copy(g_hbm.at[part], g.at[part], in_sem.at[4 + n])
        for n, part in enumerate(ghost_parts())
    ]
    chunks = []
    for n, (low, high) in enumerate(((16, 40), (40, 56), (56, 72), (72, 80))):
        part = (slice(None), pl.ds(1, TILES), pl.ds(low, high - low))
        chunks.append(pltpu.make_async_copy(g_hbm.at[part], g.at[part], in_sem.at[n]))
    chunks[0].start()
    for copy in rims:
        copy.start()
    for copy in chunks[1:]:
        copy.start()
    small = [
        pltpu.make_async_copy(conc_hbm, conc, in_sem.at[24]),
        pltpu.make_async_copy(pot_hbm, pot, in_sem.at[25]),
    ]
    for copy in small:
        copy.start()
    others = [
        pltpu.make_async_copy(conc, conc_out, out_sem.at[4]),
        pltpu.make_async_copy(pot, pot_out, out_sem.at[5]),
    ]
    for copy in rims:
        copy.wait()
    outs = []
    for n in range(4):
        chunks[n].wait()
        for step in (2 * n, 2 * n + 1):
            stream(g, f, EDGE + 8 * step, pl.ds(8 * step, 8), range(1, TILES + 1), None)
        part = (slice(None), pl.ds(16 * n, 16))
        outs.append(pltpu.make_async_copy(f.at[part], pop_out.at[part], out_sem.at[n]))
        outs[-1].start()
        if n == 0:
            for copy in small:
                copy.wait()
            for copy in others:
                copy.start()
    for copy in outs + others:
        copy.wait()


def local(populations, concentration, potential, mobility, solid_mask, block_col):
    anywhere = pl.BlockSpec(memory_space=pl.ANY)
    f32 = jnp.float32

    def field(*lead):
        return pltpu.VMEM(lead + (NT, NR, LANES), f32)

    def bare(*lead):
        return pltpu.VMEM(lead + (TILES, ROWS, LANES), f32)

    def vm(*shape):
        return pltpu.VMEM(shape + (LANES,), f32)

    scratch = [
        pltpu.VMEM((Q, ROWS, TILES * LANES), f32), field(Q),
        field(), field(), field(), bare(), field(), field(), bare(), bare(), field(),
        field(), field(), field(), field(), field(), field(), bare(),
        pltpu.VMEM((TILES, ROWS, LANES), jnp.int32),
        field(), field(), bare(), bare(), bare(), bare(), bare(),
        bare(), bare(), bare(), bare(), bare(), bare(),
        vm(2, N_DEV, 1),
        vm(2, 1, ROWS), vm(2, 2, 1, STRIP), vm(2, 4, 8), vm(2, 2, 4, 8),
        vm(2, 2, ROWS), vm(2, 2, 2, STRIP), vm(2, 5, 8), vm(2, 2, 5, 8),
        vm(2, 1, 8), vm(2, 2, 1, STRIP), vm(2, 2, 1, 8),
        vm(2, 4, ROWS), vm(1, 2, 4, STRIP), vm(2, 10, 8), vm(1, 2, 10, 8),
        pltpu.SemaphoreType.DMA((48,)),
        pltpu.SemaphoreType.DMA((48,)),
        pltpu.SemaphoreType.DMA,
        pltpu.SemaphoreType.DMA((2,)),
        pltpu.SemaphoreType.DMA((8,)), pltpu.SemaphoreType.DMA((2, 8)),
        pltpu.SemaphoreType.DMA((8,)), pltpu.SemaphoreType.DMA((2, 8)),
        pltpu.SemaphoreType.DMA((8,)), pltpu.SemaphoreType.DMA((2, 8)),
        pltpu.SemaphoreType.DMA((8,)), pltpu.SemaphoreType.DMA((1, 8)),
    ]
    flat = (ROWS, TILES * LANES)
    g_last, conc, pot = pl.pallas_call(
        kernel,
        out_shape=(
            jax.ShapeDtypeStruct((Q, NT, NR, LANES), f32),
            jax.ShapeDtypeStruct((2,) + flat, f32),
            jax.ShapeDtypeStruct(flat, f32),
        ),
        in_specs=[pl.BlockSpec(memory_space=pltpu.SMEM)] + [anywhere] * 5,
        out_specs=(anywhere,) * 3,
        scratch_shapes=scratch,
        compiler_params=pltpu.CompilerParams(
            collective_id=0, has_side_effects=True, vmem_limit_bytes=VMEM_LIMIT
        ),
        cost_estimate=pl.CostEstimate(
            flops=100_000_000, bytes_accessed=12_000_000, transcendentals=0
        ),
    )(
        block_col,
        populations.reshape((Q,) + flat),
        concentration.reshape((2,) + flat),
        potential.reshape(flat),
        mobility.reshape(flat),
        solid_mask.reshape(flat),
    )
    pop, conc, pot = pl.pallas_call(
        last_kernel,
        out_shape=(
            jax.ShapeDtypeStruct((Q,) + flat, f32),
            jax.ShapeDtypeStruct((2,) + flat, f32),
            jax.ShapeDtypeStruct(flat, f32),
        ),
        in_specs=[anywhere] * 3,
        out_specs=(anywhere,) * 3,
        scratch_shapes=[
            pltpu.VMEM((Q, NT, NR, LANES), f32),
            pltpu.VMEM((Q,) + flat, f32),
            pltpu.VMEM((2,) + flat, f32),
            pltpu.VMEM(flat, f32),
            pltpu.SemaphoreType.DMA((26,)),
            pltpu.SemaphoreType.DMA((6,)),
        ],
        compiler_params=pltpu.CompilerParams(vmem_limit_bytes=VMEM_LIMIT),
        cost_estimate=pl.CostEstimate(
            flops=10_000_000, bytes_accessed=12_000_000, transcendentals=0
        ),
    )(g_last, conc, pot)
    return (
        pop.reshape(populations.shape),
        conc.reshape(concentration.shape),
        pot.reshape(potential.shape),
    )


def solution(mesh):
    split = ("gx", "gy")
    return jax.shard_map(
        local,
        mesh=mesh,
        in_specs=(
            P(None, split, None, None),
            P(None, split, None, None),
            P(split, None, None),
            P(split, None, None),
            P(split, None, None),
            P(),
        ),
        out_specs=(P(None, split, None, None), P(None, split, None, None), P(split, None, None)),
        check_vma=False,
    )
```

```python
import jax
import jax.numpy as jnp
from jax import lax
from jax.experimental import pallas as pl
from jax.experimental.pallas import tpu as pltpu
from jax.sharding import PartitionSpec as P

BS = 32
Q = 19
STEPS = 4
N_GX = 16
N_GY = 8
N_DEV = N_GX * N_GY
VELOCITY = (
    (0, 0, 0),
    (1, 0, 0),
    (-1, 0, 0),
    (0, 1, 0),
    (0, -1, 0),
    (0, 0, 1),
    (0, 0, -1),
    (1, 1, 0),
    (-1, -1, 0),
    (1, -1, 0),
    (-1, 1, 0),
    (1, 0, 1),
    (-1, 0, -1),
    (1, 0, -1),
    (-1, 0, 1),
    (0, 1, 1),
    (0, -1, -1),
    (0, 1, -1),
    (0, -1, 1),
)
OPPOSITE = (0, 2, 1, 4, 3, 6, 5, 8, 7, 10, 9, 12, 11, 14, 13, 16, 15, 18, 17)
UP_Y = (3, 7, 10, 15, 17)
DOWN_Y = (4, 8, 9, 16, 18)
UP_X = (1, 7, 9, 11, 13)
DOWN_X = (2, 8, 10, 12, 14)
RELAX_TIME = 0.8
SCREENING = 0.5
APPLIED = 0.4
ION_STEP = 0.05
FORCE_SCALE = 0.5

MESH = pl.DeviceIdType.MESH
LANES = 128
TILES = 8
ROWS = 64
EDGE = 16
NR = ROWS + 2 * EDGE
NT = TILES + 2
VMEM_LIMIT = 60 * 1024 * 1024
UNROLL_APPLY = 4
UNROLL_BORDER = 3
UNROLL_INSIDE = 2
UNROLL_LBM = 2
SIDE = 40
STRIP = ROWS + 2 * SIDE


def tile_offsets():
    hops = lambda a: min(a, 4 - a)
    offs = [
        (a, b, c, d)
        for a in range(4)
        for b in range(4)
        for c in range(4)
        for d in range(2)
        if a + b + c + d
    ]
    offs.sort(key=lambda o: -(hops(o[0]) + hops(o[1]) + hops(o[2]) + 0.1 * o[3]))
    return offs


def stream(g, f, r, own, tiles, sink):
    lane = lax.broadcasted_iota(jnp.int32, (8, LANES), 1)
    depth = lane % BS
    group = lane // BS

    def pull(q, j):
        return g[q, j, pl.ds(r - VELOCITY[q][0], 8), :]

    caches = {q: {} for q in range(Q)}
    for j in tiles:
        pop = []
        for q in range(Q):
            _, sy, sz = VELOCITY[q]
            if sy == 0:
                v = pull(q, j)
                if sz:
                    v = pltpu.roll(v, sz % LANES, 1)
            else:
                cache = caches[q]
                for k in (j, j - sy):
                    if k not in cache:
                        cache[k] = pltpu.roll(pull(q, k), (sy * BS + sz) % LANES, 1)
                v = jnp.where(group > 0 if sy > 0 else group < 3, cache[j], cache[j - sy])
            if sz:
                wall = depth == (0 if sz > 0 else BS - 1)
                v = jnp.where(wall, g[OPPOSITE[q], j, pl.ds(r, 8), :], v)
            f[q, own, (j - 1) * LANES : j * LANES] = v
            pop.append(v)
        if sink is not None:
            sink(pop, j)


def kernel(
    col_ref, pop_hbm, conc_hbm, pot_hbm, mob_hbm, mask_hbm,
    g_out, conc_out, pot_out,
    f, g, phi, r0, w, aw, c0, c1, n0, n1, t, kx, ky, kym, kz, kzm, dg, fl, mk,
    ux, uy, uz, rho, rinv, vx, vy, dy0, dy1, dz0, dz1, slope, r_next,
    ar, sy_r, ry_r, sx_r, rx_r, sy_g, ry_g, sx_g, rx_g, sx_u, ry_u, rx_u, sy_i, ry_i, sx_i, rx_i,
    in_sem, out_sem, ar_send, ar_recv, send_r, recv_r, send_g, recv_g, send_u, recv_u,
    send_i, recv_i,
):
    gx = lax.axis_index("gx")
    gy = lax.axis_index("gy")
    right = lax.rem(gx + 1, N_GX)
    left = lax.rem(gx + N_GX - 1, N_GX)
    above = lax.rem(gy + 1, N_GY)
    below = lax.rem(gy + N_GY - 1, N_GY)
    me = gx * N_GY + gy

    lane = lax.broadcasted_iota(jnp.int32, (8, LANES), 1)
    depth = lane % BS
    group = lane // BS
    z_first = depth == 0
    z_last = depth == BS - 1

    x4, y4 = gx // 4, lax.rem(gx, 4)
    z4, core = gy // 2, lax.rem(gy, 2)
    to_gx = {
        (a, b): lax.rem(x4 + a, 4) * 4 + lax.rem(y4 + b, 4) for a in range(4) for b in range(4)
    }
    to_gy = {
        (d, e): lax.rem(z4 + d, 4) * 2 + lax.rem(core + e, 2) for d in range(4) for e in range(2)
    }

    barrier = pltpu.get_barrier_semaphore()
    for a, b, d, e in tile_offsets():
        pl.semaphore_signal(
            barrier, inc=1, device_id=(to_gx[a, b], to_gy[d, e]), device_id_type=MESH
        )

    loads = []
    for j in range(TILES):
        lanes = pl.ds(j * LANES, LANES)
        rows = pl.ds(EDGE, ROWS)
        loads.append((mob_hbm.at[:, lanes], t.at[1 + j, rows, :]))
        loads.append((mask_hbm.at[:, lanes], mk.at[j]))
        loads.append((pot_hbm.at[:, lanes], phi.at[1 + j, rows, :]))
        loads.append((conc_hbm.at[0, :, lanes], c0.at[1 + j, rows, :]))
        loads.append((conc_hbm.at[1, :, lanes], c1.at[1 + j, rows, :]))
    first = [pltpu.make_async_copy(s, d, in_sem.at[n]) for n, (s, d) in enumerate(loads)]
    pops = [pltpu.make_async_copy(pop_hbm, f, in_sem.at[len(first)])]
    for copy in first:
        copy.start()
    for copy in pops:
        copy.start()

    def exchange(par, strip_src, strip_dst, x_src, x_dst, send, recv):
        copies = []
        for to_y, dst_side in ((below, 1), (above, 0)):
            src_side = 1 - dst_side
            for to_x, src_row, dst_row, count in (
                (gx, 0, SIDE, ROWS),
                (right, ROWS - SIDE, 0, SIDE),
                (left, 0, SIDE + ROWS, SIDE),
            ):
                copies.append(
                    (
                        strip_src(src_side, src_row, count),
                        strip_dst.at[par, dst_side, :, pl.ds(dst_row, count), :],
                        (to_x, to_y),
                    )
                )
        copies.append((x_src.at[1], x_dst.at[par, 0], (right, gy)))
        copies.append((x_src.at[0], x_dst.at[par, 1], (left, gy)))
        return [
            pltpu.make_async_remote_copy(
                src_ref=s, dst_ref=d, send_sem=send.at[k], recv_sem=recv.at[par, k],
                device_id=dev, device_id_type=MESH,
            )
            for k, (s, d, dev) in enumerate(copies)
        ]

    def staged(ref):
        return lambda side, row, count: ref.at[side, :, pl.ds(row, count), :]

    def ex_r(par):
        return exchange(par, staged(sy_r), ry_r, sx_r, rx_r, send_r, recv_r)

    def ex_g(par):
        return exchange(par, staged(sy_g), ry_g, sx_g, rx_g, send_g, recv_g)

    def ex_u(par):
        def src(side, row, count):
            tile = TILES if side == 1 else 1
            return uy.at[pl.ds(tile, 1), pl.ds(EDGE + row, count), :]

        return exchange(par, src, ry_u, sx_u, rx_u, send_u, recv_u)

    def start(copies):
        for copy in copies:
            copy.start()

    def finish(copies):
        for copy in copies:
            copy.wait()

    here = col_ref[2 * gy]
    ahead = [
        jnp.broadcast_to(here - col_ref[2 * other], (8, LANES)) for other in (below, above)
    ]
    less = [v < 0 for v in ahead]
    more = [v > 0 for v in ahead]

    def strip_rows(ref, par, side, number, k):
        first, same, last = [
            ref[par, side, number, pl.ds(start + 8 * k, 8), :] for start in (0, BS, 2 * BS)
        ]
        return jnp.where(less[side], first, jnp.where(more[side], last, same))

    def own_rows(step):
        return pl.multiple_of(EDGE + 8 * step, 8)

    def rolled(v, shift):
        return pltpu.roll(v, shift % LANES, 1)

    def y_next(load, tile, cache, top=NT - 1):
        for k in (tile, min(tile + 1, top)):
            if k not in cache:
                cache[k] = rolled(load(k), -BS)
        if tile == top:
            return cache[tile]
        return jnp.where(group < 3, cache[tile], cache[tile + 1])

    def y_prev(load, tile, cache, bottom=0):
        for k in (max(tile - 1, bottom), tile):
            if k not in cache:
                cache[k] = rolled(load(k), BS)
        if tile == bottom:
            return cache[tile]
        return jnp.where(group > 0, cache[tile], cache[tile - 1])

    def loader(ref, rows):
        return lambda j: ref[j, rows, :]

    def apply(ref, r, tiles, sink):
        rows = pl.ds(r, 8)
        load = loader(ref, rows)
        up = {}
        down = {}
        for j in tiles:
            here_v = load(j)
            out = dg[j, rows, :] * here_v
            out = out - kx[j, rows, :] * ref[j, pl.ds(r + 1, 8), :]
            out = out - kx[j, pl.ds(r - 1, 8), :] * ref[j, pl.ds(r - 1, 8), :]
            out = out - ky[j, rows, :] * y_next(load, j, up)
            out = out - kym[j, rows, :] * y_prev(load, j, down)
            out = out - kz[j, rows, :] * rolled(here_v, -1)
            out = out - kzm[j, rows, :] * rolled(here_v, 1)
            sink(j, here_v, out)

    OWN = list(range(1, TILES + 1))
    ALL = list(range(NT))

    def border(work):
        @pl.loop(0, 2, unroll=True)
        def _(k):
            work(7 * k, OWN)

        @pl.loop(1, 7, unroll=UNROLL_BORDER)
        def _(step):
            work(step, OWN[:1])
            work(step, OWN[-1:])

    def inside(work):
        @pl.loop(1, 7, unroll=UNROLL_INSIDE)
        def _(step):
            work(step, OWN[1:-1])

    def rim(work):
        @pl.loop(0, 2, unroll=True)
        def _(k):
            work(7 * k, ALL)

        @pl.loop(1, 7, unroll=UNROLL_BORDER)
        def _(step):
            work(step, ALL[:2])
            work(step, ALL[-2:])

    def rows_beyond(work, tiles=OWN):
        @pl.loop(0, 2, unroll=True)
        def _(k):
            work(9 * k - 1, tiles)

    def to_w(tau):
        def work(step, tiles):
            r = own_rows(step)

            def sink(j, here_v, out):
                w[j, pl.ds(r, 8), :] = out - tau * here_v

            apply(r0, r, tiles, sink)

        return work

    def moments(pop):
        p = pop
        xp = p[7] + p[9] + p[11] + p[13] + p[1]
        xm = p[8] + p[10] + p[12] + p[14] + p[2]
        yp = p[15] + p[17] + p[3]
        ym = p[16] + p[18] + p[4]
        density = p[0] + xp + xm + yp + ym + (p[5] + p[6])
        jx = xp - xm
        jy = (yp - ym) + ((p[7] + p[10]) - (p[8] + p[9]))
        jz = (p[5] - p[6]) + ((p[11] + p[14]) - (p[12] + p[13])) + (
            (p[15] + p[18]) - (p[16] + p[17])
        )
        inverse = 1.0 / density
        return density, inverse, jx * inverse, jy * inverse, jz * inverse

    def store_moments(pop, j, r):
        density, inverse, a, b, d = moments(pop)
        rows = pl.ds(r, 8)
        own = pl.ds(pl.multiple_of(r - EDGE, 8), 8)
        rho[j - 1, own, :] = density
        rinv[j - 1, own, :] = inverse
        ux[j, rows, :] = a
        uy[j, rows, :] = b
        uz[j - 1, own, :] = d

    def send_velocity(par):
        for j in OWN:
            sx_u[0, 0, pl.ds(j - 1, 1), :] = ux[j, pl.ds(EDGE, 1), :]
            sx_u[1, 0, pl.ds(j - 1, 1), :] = ux[j, pl.ds(EDGE + ROWS - 1, 1), :]
        start(ex_u(par))

    def take_velocity(par):
        finish(ex_u(par))
        for j in OWN:
            ux[j, pl.ds(EDGE - 1, 1), :] = rx_u[par, 0, 0, pl.ds(j - 1, 1), :]
            ux[j, pl.ds(EDGE + ROWS, 1), :] = rx_u[par, 1, 0, pl.ds(j - 1, 1), :]
        for k in range(10):
            rows = pl.ds(EDGE - 8 + 8 * k, 8)
            uy[0, rows, :] = strip_rows(ry_u, par, 0, 0, k)
            uy[NT - 1, rows, :] = strip_rows(ry_u, par, 1, 0, k)

    def send_residual(par):
        for k in range(8):
            out = pl.ds(8 * k, 8)
            a = rolled(n0[0, out, :], 2 * BS)
            b = rolled(n1[0, out, :], 3 * BS)
            sy_r[0, 0, out, :] = jnp.where(
                group < 2, r_next[0, out, :], jnp.where(group == 2, a, b)
            )
            a = rolled(n0[TILES - 1, out, :], BS)
            b = rolled(n1[TILES - 1, out, :], 2 * BS)
            sy_r[1, 0, out, :] = jnp.where(
                group > 1, r_next[TILES - 1, out, :], jnp.where(group == 0, a, b)
            )
        for k in range(TILES):
            to = pl.ds(k, 1)
            for side, row, ahead in ((0, 0, 1), (1, ROWS - 1, -1)):
                sx_r[side, 0, to, :] = r_next[k, pl.ds(row, 1), :]
                sx_r[side, 1, to, :] = r_next[k, pl.ds(row + ahead, 1), :]
                sx_r[side, 2, to, :] = n0[k, pl.ds(row, 1), :]
                sx_r[side, 3, to, :] = n1[k, pl.ds(row, 1), :]
        start(ex_r(par))

    def take_residual(par):
        finish(ex_r(par))
        for k in range(10):
            rows = pl.ds(EDGE - 8 + 8 * k, 8)
            v = strip_rows(ry_r, par, 0, 0, k)
            r0[0, rows, :] = v
            c0[0, rows, :] = rolled(v, 3 * BS)
            c1[0, rows, :] = rolled(v, 2 * BS)
            v = strip_rows(ry_r, par, 1, 0, k)
            r0[NT - 1, rows, :] = v
            c0[NT - 1, rows, :] = rolled(v, 2 * BS)
            c1[NT - 1, rows, :] = rolled(v, BS)
        for j in OWN:
            at = pl.ds(j - 1, 1)
            last = EDGE + ROWS - 1
            r0[j, pl.ds(EDGE - 1, 1), :] = rx_r[par, 0, 0, at, :]
            r0[j, pl.ds(EDGE - 2, 1), :] = rx_r[par, 0, 1, at, :]
            r0[j, pl.ds(last + 1, 1), :] = rx_r[par, 1, 0, at, :]
            r0[j, pl.ds(last + 2, 1), :] = rx_r[par, 1, 1, at, :]
            for s, ref in enumerate((c0, c1)):
                ref[j, pl.ds(EDGE - 1, 1), :] = rx_r[par, 0, 2 + s, at, :]
                ref[j, pl.ds(last + 1, 1), :] = rx_r[par, 1, 2 + s, at, :]

    def send_populations(par):
        for side, tile, names in ((0, 1, DOWN_Y), (1, TILES, UP_Y)):
            home = 0 if side == 0 else 3
            for k in range(8):
                rows = pl.ds(EDGE + 8 * k, 8)
                out = pl.ds(8 * k, 8)
                parts = [
                    rolled(g[q, tile, rows, :], (at % 4 - home) * BS)
                    for at, q in enumerate(names)
                ]
                sy_g[side, 0, out, :] = jnp.where(
                    group == 0, parts[0],
                    jnp.where(group == 1, parts[1], jnp.where(group == 2, parts[2], parts[3])),
                )
                sy_g[side, 1, out, :] = parts[4]
        for side, row, names in ((0, EDGE, DOWN_X), (1, EDGE + ROWS - 1, UP_X)):
            for at, q in enumerate(names):
                for j in OWN:
                    sx_g[side, at, pl.ds(j - 1, 1), :] = g[q, j, pl.ds(row, 1), :]
        start(ex_g(par))

    def take_populations(par):
        finish(ex_g(par))
        for side, tile, names in ((0, 0, UP_Y), (1, NT - 1, DOWN_Y)):
            home = 3 if side == 0 else 0
            for k in range(10):
                rows = pl.ds(EDGE - 8 + 8 * k, 8)
                v = strip_rows(ry_g, par, side, 0, k)
                for at, q in enumerate(names):
                    if at == 4:
                        v = strip_rows(ry_g, par, side, 1, k)
                    g[q, tile, rows, :] = rolled(v, (home - at % 4) * BS)
        for side, row, names in ((0, EDGE - 1, UP_X), (1, EDGE + ROWS, DOWN_X)):
            for at, q in enumerate(names):
                for j in OWN:
                    g[q, j, pl.ds(row, 1), :] = rx_g[par, side, at, pl.ds(j - 1, 1), :]

    def propagate(step, tiles):
        r = own_rows(step)
        own = pl.ds(pl.multiple_of(8 * step, 8), 8)
        stream(g, f, r, own, tiles, lambda pop, j: store_moments(pop, j, r))

    def collide(step, tiles):
        r = own_rows(step)
        own = pl.ds(pl.multiple_of(8 * step, 8), 8)
        rows = pl.ds(r, 8)
        for j in tiles:
            k = j - 1
            fluid = fl[k, own, :] > 0.0
            density = rho[k, own, :]
            a = vx[k, own, :]
            b = vy[k, own, :]
            d = uz[k, own, :]
            square = a * a + b * b + d * d
            rest = 1.25 - 1.875 * square
            big = density * (1.0 / 18.0)
            small = density * (1.0 / 36.0)
            lanes = slice(k * LANES, j * LANES)
            pop0 = f[0, own, lanes]
            relaxed = density * (1.0 / 3.0) * rest - 0.25 * pop0
            g[0, j, rows, :] = jnp.where(fluid, relaxed, pop0)
            for q in range(1, Q, 2):
                cx, cy, cz = VELOCITY[q]
                s = None
                for comp, val in ((cx, a), (cy, b), (cz, d)):
                    if comp:
                        if s is None:
                            s = val
                        else:
                            s = s + val if comp > 0 else s - val
                weight = big if q < 7 else small
                even = weight * (rest + 5.625 * (s * s))
                odd = weight * (3.75 * s)
                fa = f[q, own, lanes]
                fb = f[q + 1, own, lanes]
                g[q, j, rows, :] = jnp.where(fluid, (even + odd) - 0.25 * fa, fb)
                g[q + 1, j, rows, :] = jnp.where(fluid, (even - odd) - 0.25 * fb, fa)

    for copy in first:
        copy.wait()

    @pl.loop(0, 8)
    def _(step):
        r = own_rows(step)
        own = pl.ds(pl.multiple_of(8 * step, 8), 8)
        for j in OWN:
            fluid = mk[j - 1, own, :] == 0
            fl[j - 1, own, :] = jnp.where(fluid, 1.0, 0.0)
            t[j, pl.ds(r, 8), :] = jnp.where(fluid, t[j, pl.ds(r, 8), :], -1.0)

    starts = (t, phi, c0, c1)
    depths = (3, 3, 2, 2)
    for j in OWN:
        at = 0
        for ref, deep in zip(starts, depths):
            for layer in range(deep):
                to = pl.ds(j - 1, 1)
                sx_i[0, at, to, :] = ref[j, pl.ds(EDGE + layer, 1), :]
                sx_i[1, at, to, :] = ref[j, pl.ds(EDGE + ROWS - 1 - layer, 1), :]
                at += 1
    for n, ref in enumerate(starts):
        for k in range(8):
            rows = pl.ds(EDGE + 8 * k, 8)
            sy_i[0, n, pl.ds(8 * k, 8), :] = ref[1, rows, :]
            sy_i[1, n, pl.ds(8 * k, 8), :] = ref[TILES, rows, :]
    first_halo = exchange(0, staged(sy_i), ry_i, sx_i, rx_i, send_i, recv_i)
    pl.semaphore_wait(barrier, N_DEV - 1)
    start(first_halo)

    def coefficients(step, tiles):
        r = own_rows(step)
        rows = pl.ds(r, 8)

        def load(j):
            return jnp.maximum(t[j, rows, :], 0.0)

        up = {}
        down = {}
        for j in tiles:
            raw = t[j, rows, :]
            v = load(j)
            fluid = jnp.where(raw >= 0.0, 1.0, 0.0)
            xn = v * jnp.maximum(t[j, pl.ds(r + 1, 8), :], 0.0)
            xp = v * jnp.maximum(t[j, pl.ds(r - 1, 8), :], 0.0)
            yn = v * y_next(load, j, up)
            yp = v * y_prev(load, j, down)
            zn = jnp.where(z_last, 0.0, v * rolled(v, -1))
            zp = jnp.where(z_first, 0.0, v * rolled(v, 1))
            kx[j, rows, :] = xn
            ky[j, rows, :] = yn
            kym[j, rows, :] = yp
            kz[j, rows, :] = zn
            kzm[j, rows, :] = zp
            diagonal = SCREENING * fluid + (1.0 - fluid)
            dg[j, rows, :] = diagonal + xn + xp + yn + yp + zn + zp

    def first_residual(step, tiles):
        r = own_rows(step)
        rows = pl.ds(r, 8)

        def sink(j, here_v, out):
            charge = c0[j, rows, :] - c1[j, rows, :]
            r0[j, rows, :] = jnp.where(t[j, rows, :] >= 0.0, charge, 0.0) - out

        apply(phi, r, tiles, sink)

    inside(coefficients)
    for copy in pops:
        copy.wait()

    @pl.loop(0, 8)
    def _(step):
        r = own_rows(step)
        own = pl.ds(pl.multiple_of(8 * step, 8), 8)
        for j in OWN:
            store_moments(
                [f[q, own, (j - 1) * LANES : j * LANES] for q in range(Q)], j, r
            )

    send_velocity(0)

    finish(first_halo)
    for k in range(10):
        rows = pl.ds(EDGE - 8 + 8 * k, 8)
        for n, ref in enumerate(starts):
            ref[0, rows, :] = strip_rows(ry_i, 0, 0, n, k)
            ref[NT - 1, rows, :] = strip_rows(ry_i, 0, 1, n, k)
    for j in OWN:
        at = 0
        for ref, deep in zip(starts, depths):
            for layer in range(deep):
                of = pl.ds(j - 1, 1)
                ref[j, pl.ds(EDGE - 1 - layer, 1), :] = rx_i[0, 0, at, of, :]
                ref[j, pl.ds(EDGE + ROWS + layer, 1), :] = rx_i[0, 1, at, of, :]
                at += 1

    rim(coefficients)
    rows_beyond(coefficients, ALL)
    rim(first_residual)
    rows_beyond(first_residual, ALL)
    inside(first_residual)

    def body(n, tau):
        par = lax.rem(n, 2)
        nxt = 1 - par
        @pl.when(n > 0)
        def _():
            take_residual(par)


        make_w = to_w(tau)
        rim(make_w)
        rows_beyond(make_w)

        zero = jnp.zeros((8, LANES), jnp.float32)

        def sums(step, acc):
            r = own_rows(step)
            own = pl.ds(pl.multiple_of(8 * step, 8), 8)
            acc = list(acc)

            def sink(j, here_v, out):
                aw[j - 1, own, :] = out
                res = r0[j, pl.ds(r, 8), :]
                acc[0] = acc[0] + res * res
                acc[1] = acc[1] + res * here_v
                acc[2] = acc[2] + here_v * here_v
                acc[3] = acc[3] + here_v * out

            apply(w, r, OWN, sink)
            return tuple(acc)

        acc = lax.fori_loop(0, 8, sums, (zero,) * 4, unroll=UNROLL_APPLY)
        rows4 = []
        for a in acc:
            a = jnp.sum(a, axis=0, keepdims=True)
            a = jnp.broadcast_to(a, (8, LANES))
            a = a + rolled(a, 2 * BS)
            rows4.append(a + rolled(a, BS))
        mine = jnp.where(
            group == 0, rows4[0],
            jnp.where(group == 1, rows4[1], jnp.where(group == 2, rows4[2], rows4[3])),
        )[0:1]
        ar[par, me] = mine
        for a, b, d, e in tile_offsets():
            dev = (to_gx[a, b], to_gy[d, e])
            pltpu.make_async_remote_copy(
                src_ref=ar.at[par, me], dst_ref=ar.at[par, me],
                send_sem=ar_send, recv_sem=ar_recv.at[par],
                device_id=dev, device_id_type=MESH,
            ).start()

        @pl.when(n > 0)
        def _():
            take_populations(nxt)
            border(propagate)
            send_velocity(par)
            inside(propagate)

        others = ar.at[par, pl.ds(0, N_DEV - 1)]
        pltpu.make_async_copy(others, others, ar_send).wait()
        pltpu.make_async_copy(others, others, ar_recv.at[par]).wait()
        parts = [ar[par, k] for k in range(8)]
        for k in range(8, N_DEV):
            parts[k % 8] = parts[k % 8] + ar[par, k]
        while len(parts) > 1:
            parts = [parts[k] + parts[k + 1] for k in range(0, len(parts), 2)]
        total = parts[0]
        where = lax.broadcasted_iota(jnp.int32, (1, LANES), 1) // BS
        s = [
            jnp.sum(jnp.where(where == k, total, 0.0), axis=1, keepdims=True) for k in range(4)
        ]
        ratio = s[1] / s[0]
        lam = tau[0:1, 0:1] + ratio
        first_len = 1.0 / lam
        square = first_len * first_len
        rr1 = square * (s[2] - ratio * ratio * s[0])
        beta = rr1 / s[0]
        curve = square * (
            ratio * ratio * lam * s[0] - 2.0 * ratio * (s[2] + tau[0:1, 0:1] * s[1]) + s[3]
        ) - beta * beta * lam * s[0]
        lam_all = jnp.broadcast_to(lam, (8, LANES))
        second_len = jnp.where(curve > 0.0, rr1 / jnp.where(curve > 0.0, curve, 1.0), 0.0)
        along_r = first_len + second_len * (first_len * ratio + beta)
        along_w = second_len * first_len
        cr = jnp.broadcast_to(along_r, (8, LANES))
        cw = jnp.broadcast_to(along_w, (8, LANES))
        keep_r = jnp.broadcast_to(1.0 - along_r * tau[0:1, 0:1], (8, LANES))

        def new_phi(r, tiles):
            rows = pl.ds(r, 8)
            new = [
                phi[j, rows, :] + (cr * r0[j, rows, :] - cw * w[j, rows, :]) for j in tiles
            ]
            for j, v in zip(tiles, new):
                phi[j, rows, :] = v

        @pl.loop(0, 8, unroll=UNROLL_APPLY)
        def _(step):
            new_phi(own_rows(step), ALL)

        new_phi(EDGE - 8, OWN)
        new_phi(EDGE + ROWS, OWN)
        take_velocity(par)

        def faces(k, ca, cb, da, db, pa, pb, ua, ub, half_field):
            hu = 0.25 * (ua + ub)
            hd = 0.5 * (pb - pa)
            if half_field:
                hd = hd - half_field
            return (
                k * ((ca - cb) + (ca + cb) * (hu - hd)),
                k * ((da - db) + (da + db) * (hu + hd)),
            )

        def y_faces(step, tiles):
            r = own_rows(step)
            rows = pl.ds(r, 8)
            own = pl.ds(pl.multiple_of(8 * step, 8), 8)
            p, a, b, v = [loader(ref, rows) for ref in (phi, c0, c1, uy)]
            caches = [{} for _ in range(8)]
            for j in tiles:
                pn, an, bn, vn = [y_next(ld, j, ca) for ld, ca in zip((p, a, b, v), caches)]
                pp, ap, bp, vp = [y_prev(ld, j, ca) for ld, ca in zip((p, a, b, v), caches[4:])]
                pj, aj, bj, vj = p(j), a(j), b(j), v(j)
                f0, f1 = faces(ky[j, rows, :], aj, an, bj, bn, pj, pn, vj, vn, 0.0)
                g0, g1 = faces(kym[j, rows, :], ap, aj, bp, bj, pp, pj, vp, vj, 0.0)
                dy0[j - 1, own, :] = f0 - g0
                dy1[j - 1, own, :] = f1 - g1
                slope[j - 1, own, :] = pn - pp

        def z_faces(step, tiles):
            rows = pl.ds(own_rows(step), 8)
            own = pl.ds(pl.multiple_of(8 * step, 8), 8)
            for j in tiles:
                here_v = (c0[j, rows, :], c1[j, rows, :], phi[j, rows, :], uz[j - 1, own, :])
                aj, bj, pj, vj = here_v
                an, bn, pn, vn = [rolled(v, -1) for v in here_v]
                ap, bp, pp, vp = [rolled(v, 1) for v in here_v]
                f0, f1 = faces(kz[j, rows, :], aj, an, bj, bn, pj, pn, vj, vn, 0.0)
                g0, g1 = faces(kzm[j, rows, :], ap, aj, bp, bj, pp, pj, vp, vj, 0.0)
                dz0[j - 1, own, :] = f0 - g0
                dz1[j - 1, own, :] = f1 - g1

        def transport_step(step, tiles):
            r = own_rows(step)
            rows = pl.ds(r, 8)
            less = pl.ds(r - 1, 8)
            more = pl.ds(r + 1, 8)
            own = pl.ds(pl.multiple_of(8 * step, 8), 8)
            for j in tiles:
                k = j - 1
                aj, bj, pj, vj = [ref[j, rows, :] for ref in (c0, c1, phi, ux)]
                an, bn, pn, vn = [ref[j, more, :] for ref in (c0, c1, phi, ux)]
                ap, bp, pp, vp = [ref[j, less, :] for ref in (c0, c1, phi, ux)]
                half = 0.5 * APPLIED
                f0, f1 = faces(kx[j, rows, :], aj, an, bj, bn, pj, pn, vj, vn, half)
                g0, g1 = faces(kx[j, less, :], ap, aj, bp, bj, pp, pj, vp, vj, half)
                d0 = f0 - g0 + dy0[k, own, :] + dz0[k, own, :]
                d1 = f1 - g1 + dy1[k, own, :] + dz1[k, own, :]
                new0 = aj - ION_STEP * d0
                new1 = bj - ION_STEP * d1
                n0[k, own, :] = new0
                n1[k, own, :] = new1
                charge = new0 - new1
                push = (FORCE_SCALE * RELAX_TIME) * charge * rinv[k, own, :]
                vx[k, own, :] = vj + push * (APPLIED - 0.5 * (pn - pp))
                vy[k, own, :] = uy[j, rows, :] - push * (0.5 * slope[k, own, :])
                r_next[k, own, :] = (
                    keep_r * r0[j, rows, :] - cr * w[j, rows, :] + cw * aw[k, own, :]
                    + fl[k, own, :] * (charge - (aj - bj))
                )

        border(y_faces)
        border(z_faces)
        border(transport_step)

        @pl.when(n < STEPS - 1)
        def _():
            send_residual(nxt)

        border(collide)
        send_populations(par)
        inside(y_faces)
        inside(z_faces)
        inside(transport_step)
        inside(collide)

        @pl.loop(0, 8, unroll=2)
        def _(step):
            rows = pl.ds(own_rows(step), 8)
            own = pl.ds(pl.multiple_of(8 * step, 8), 8)
            for j in OWN:
                c0[j, rows, :] = n0[j - 1, own, :]
                c1[j, rows, :] = n1[j - 1, own, :]
                r0[j, rows, :] = r_next[j - 1, own, :]

        inside(to_w(lam_all))
        return lam_all

    one = jnp.ones((8, LANES), jnp.float32)
    inside(to_w(one))
    lax.fori_loop(0, STEPS, body, one)

    own = pl.ds(EDGE, ROWS)
    out = [(g.at[:, pl.ds(1, TILES), own, :], g_out.at[:, pl.ds(1, TILES), own, :])]
    for j in range(TILES):
        lanes = pl.ds(j * LANES, LANES)
        out.append((phi.at[1 + j, own, :], pot_out.at[:, lanes]))
        out.append((c0.at[1 + j, own, :], conc_out.at[0, :, lanes]))
        out.append((c1.at[1 + j, own, :], conc_out.at[1, :, lanes]))
    done = [pltpu.make_async_copy(s, d, out_sem.at[n]) for n, (s, d) in enumerate(out)]
    start(done)
    take_populations((STEPS - 1) % 2)
    rims = [
        pltpu.make_async_copy(g.at[part], g_out.at[part], out_sem.at[len(done) + n])
        for n, part in enumerate(ghost_parts())
    ]
    start(rims)
    finish(done + rims)


def ghost_parts():
    parts = [(q, pl.ds(0, 1), pl.ds(EDGE - 8, ROWS + 16)) for q in UP_Y]
    parts += [(q, pl.ds(NT - 1, 1), pl.ds(EDGE - 8, ROWS + 16)) for q in DOWN_Y]
    parts += [(q, pl.ds(1, TILES), pl.ds(EDGE - 8, 8)) for q in UP_X]
    parts += [(q, pl.ds(1, TILES), pl.ds(EDGE + ROWS, 8)) for q in DOWN_X]
    return parts


def last_kernel(
    g_hbm, conc_hbm, pot_hbm, pop_out, conc_out, pot_out, g, f, conc, pot, in_sem, out_sem
):
    rims = [
        pltpu.make_async_copy(g_hbm.at[part], g.at[part], in_sem.at[4 + n])
        for n, part in enumerate(ghost_parts())
    ]
    chunks = []
    for n, (low, high) in enumerate(((16, 40), (40, 56), (56, 72), (72, 80))):
        part = (slice(None), pl.ds(1, TILES), pl.ds(low, high - low))
        chunks.append(pltpu.make_async_copy(g_hbm.at[part], g.at[part], in_sem.at[n]))
    chunks[0].start()
    for copy in rims:
        copy.start()
    for copy in chunks[1:]:
        copy.start()
    small = [
        pltpu.make_async_copy(conc_hbm, conc, in_sem.at[24]),
        pltpu.make_async_copy(pot_hbm, pot, in_sem.at[25]),
    ]
    for copy in small:
        copy.start()
    others = [
        pltpu.make_async_copy(conc, conc_out, out_sem.at[4]),
        pltpu.make_async_copy(pot, pot_out, out_sem.at[5]),
    ]
    for copy in rims:
        copy.wait()
    outs = []
    for n in range(4):
        chunks[n].wait()
        for step in (2 * n, 2 * n + 1):
            stream(g, f, EDGE + 8 * step, pl.ds(8 * step, 8), range(1, TILES + 1), None)
        part = (slice(None), pl.ds(16 * n, 16))
        outs.append(pltpu.make_async_copy(f.at[part], pop_out.at[part], out_sem.at[n]))
        outs[-1].start()
        if n == 0:
            for copy in small:
                copy.wait()
            for copy in others:
                copy.start()
    for copy in outs + others:
        copy.wait()


def local(populations, concentration, potential, mobility, solid_mask, block_col):
    anywhere = pl.BlockSpec(memory_space=pl.ANY)
    f32 = jnp.float32

    def field(*lead):
        return pltpu.VMEM(lead + (NT, NR, LANES), f32)

    def bare(*lead):
        return pltpu.VMEM(lead + (TILES, ROWS, LANES), f32)

    def vm(*shape):
        return pltpu.VMEM(shape + (LANES,), f32)

    scratch = [
        pltpu.VMEM((Q, ROWS, TILES * LANES), f32), field(Q),
        field(), field(), field(), bare(), field(), field(), bare(), bare(), field(),
        field(), field(), field(), field(), field(), field(), bare(),
        pltpu.VMEM((TILES, ROWS, LANES), jnp.int32),
        field(), field(), bare(), bare(), bare(), bare(), bare(),
        bare(), bare(), bare(), bare(), bare(), bare(),
        vm(2, N_DEV, 1),
        vm(2, 1, ROWS), vm(2, 2, 1, STRIP), vm(2, 4, 8), vm(2, 2, 4, 8),
        vm(2, 2, ROWS), vm(2, 2, 2, STRIP), vm(2, 5, 8), vm(2, 2, 5, 8),
        vm(2, 1, 8), vm(2, 2, 1, STRIP), vm(2, 2, 1, 8),
        vm(2, 4, ROWS), vm(1, 2, 4, STRIP), vm(2, 10, 8), vm(1, 2, 10, 8),
        pltpu.SemaphoreType.DMA((48,)),
        pltpu.SemaphoreType.DMA((48,)),
        pltpu.SemaphoreType.DMA,
        pltpu.SemaphoreType.DMA((2,)),
        pltpu.SemaphoreType.DMA((8,)), pltpu.SemaphoreType.DMA((2, 8)),
        pltpu.SemaphoreType.DMA((8,)), pltpu.SemaphoreType.DMA((2, 8)),
        pltpu.SemaphoreType.DMA((8,)), pltpu.SemaphoreType.DMA((2, 8)),
        pltpu.SemaphoreType.DMA((8,)), pltpu.SemaphoreType.DMA((1, 8)),
    ]
    flat = (ROWS, TILES * LANES)
    g_last, conc, pot = pl.pallas_call(
        kernel,
        out_shape=(
            jax.ShapeDtypeStruct((Q, NT, NR, LANES), f32),
            jax.ShapeDtypeStruct((2,) + flat, f32),
            jax.ShapeDtypeStruct(flat, f32),
        ),
        in_specs=[pl.BlockSpec(memory_space=pltpu.SMEM)] + [anywhere] * 5,
        out_specs=(anywhere,) * 3,
        scratch_shapes=scratch,
        compiler_params=pltpu.CompilerParams(
            collective_id=0, has_side_effects=True, vmem_limit_bytes=VMEM_LIMIT
        ),
        cost_estimate=pl.CostEstimate(
            flops=100_000_000, bytes_accessed=12_000_000, transcendentals=0
        ),
    )(
        block_col,
        populations.reshape((Q,) + flat),
        concentration.reshape((2,) + flat),
        potential.reshape(flat),
        mobility.reshape(flat),
        solid_mask.reshape(flat),
    )
    pop, conc, pot = pl.pallas_call(
        last_kernel,
        out_shape=(
            jax.ShapeDtypeStruct((Q,) + flat, f32),
            jax.ShapeDtypeStruct((2,) + flat, f32),
            jax.ShapeDtypeStruct(flat, f32),
        ),
        in_specs=[anywhere] * 3,
        out_specs=(anywhere,) * 3,
        scratch_shapes=[
            pltpu.VMEM((Q, NT, NR, LANES), f32),
            pltpu.VMEM((Q,) + flat, f32),
            pltpu.VMEM((2,) + flat, f32),
            pltpu.VMEM(flat, f32),
            pltpu.SemaphoreType.DMA((26,)),
            pltpu.SemaphoreType.DMA((6,)),
        ],
        compiler_params=pltpu.CompilerParams(vmem_limit_bytes=VMEM_LIMIT),
        cost_estimate=pl.CostEstimate(
            flops=10_000_000, bytes_accessed=12_000_000, transcendentals=0
        ),
    )(g_last, conc, pot)
    return (
        pop.reshape(populations.shape),
        conc.reshape(concentration.shape),
        pot.reshape(potential.shape),
    )


def solution(mesh):
    split = ("gx", "gy")
    return jax.shard_map(
        local,
        mesh=mesh,
        in_specs=(
            P(None, split, None, None),
            P(None, split, None, None),
            P(split, None, None),
            P(split, None, None),
            P(split, None, None),
            P(),
        ),
        out_specs=(P(None, split, None, None), P(None, split, None, None), P(split, None, None)),
        check_vma=False,
    )
```
